128 devices in a mesh: ctx: 4 (over y), exp: 32 (over z, x, core).
Axes of the slice: x: 4, y: 4, z: 4, core: 2. Of those that a mesh axis runs over, the one named last changes fastest.
Arguments:
- queries: bfloat16 [4096, 2, 4096], P('ctx', None, 'exp'), may hold values from -8 to 8
- key_rows: bfloat16 [4096, 2, 256], P(('ctx', 'exp')), may hold values from -8 to 8
- values: bfloat16 [4096, 2, 256], P(('ctx', 'exp')), may hold values from -6 to 6
- hidden: bfloat16 [4096, 2, 4096], P(('ctx', 'exp')), may hold values from -6 to 6
- norm_gain: float32 [4096], replicated, may hold values from 0.5 to 2
- routes: int32 [4096, 2, 8], P(('ctx', 'exp')), may hold values from 0 to 127, all different within a row
- route_gates: float32 [4096, 2, 8], P(('ctx', 'exp')), may hold values from 0.02 to 0.3
- expert_home: int32 [128], replicated, may hold values from 0 to 127, each once
- w_gate: bfloat16 [128, 4096, 768], P(('ctx', 'exp')), may hold values from -0.09375 to 0.09375
- w_up: bfloat16 [128, 4096, 768], P(('ctx', 'exp')), may hold values from -0.09375 to 0.09375
- w_down: bfloat16 [128, 768, 4096], P(('ctx', 'exp')), may hold values from -0.21875 to 0.21875
Outputs:
- context: bfloat16 [4096, 2, 4096], P('ctx', None, 'exp')
- layer_out: bfloat16 [4096, 2, 4096], P(('ctx', 'exp'))
The draws below stay inside these ranges and needn't reach their ends.
Inputs may be any that keep to these rules, and one draw needn't show every extreme that they name: `routes`: each token names 8 different experts. `expert_home`: a permutation of the 128 experts.
All inputs are finite; a program needn't handle non-finite values.
Results may differ from the reference program's by a relative error of at most 0.0045.
Values may be sent and summed in bfloat16 or wider, within the bound.
A program may use at most 128 MiB of HBM per device.

```python
import math
import jax
import jax.numpy as jnp
from jax import lax

D = 4096
QUERY_HEADS = 32
KEY_VALUE_HEADS = 2
HEAD_WIDTH = 128
FF = 768
TOPK = 8
SEQUENCE_COUNT = 2
SEQUENCE_LENGTH = 4096
TOK_DEV = 64
EXPERTS = 128
CAP = 3
N_CTX = 4
N_EXP = 32


def draw_queries(key, part):
    key = jax.random.fold_in(key, 5)
    array_shape = (SEQUENCE_LENGTH, SEQUENCE_COUNT, QUERY_HEADS * HEAD_WIDTH)
    return jnp.clip(jax.random.normal(key, array_shape, jnp.float32), -6.0, 6.0).astype(jnp.bfloat16)


def draw_key_rows(key, part):
    key = jax.random.fold_in(key, 9)
    array_shape = (SEQUENCE_LENGTH, SEQUENCE_COUNT, KEY_VALUE_HEADS * HEAD_WIDTH)
    return jnp.clip(jax.random.normal(key, array_shape, jnp.float32), -6.0, 6.0).astype(jnp.bfloat16)


def level_of(rng, extent, cuts, low, high):
    loudness = 1.0
    for axis_at, shards_of in cuts:
        steps = jax.random.uniform(jax.random.fold_in(jax.random.fold_in(rng, 6), axis_at), (shards_of,), jnp.float32, low / len(cuts), high / len(cuts))
        loudness = loudness * jnp.repeat(jnp.exp(steps), extent[axis_at] // shards_of).reshape((-1,) + (1,) * (len(extent) - 1 - axis_at))
    return loudness


def choose_distinct(stream_key, rows, number_of, top, lift):
    ranking = jax.random.permutation(jax.random.fold_in(stream_key, 1), number_of)
    boost = ranking
    for power in range(3):
        boost = boost * boost // number_of
    boost = boost * lift // number_of
    tickets = jax.random.randint(jax.random.fold_in(stream_key, 2), (rows, number_of), 0, 4096) + boost
    fixed_rows = jax.random.permutation(jax.random.fold_in(stream_key, 3), rows)[jnp.arange(number_of) % rows]
    tickets = jnp.where(jnp.arange(rows)[:, None] == fixed_rows[None, :], 1 << 14, tickets)
    score = tickets * number_of + jnp.arange(number_of)
    return lax.top_k(score.astype(jnp.int32), top)[1].astype(jnp.int32)


def normal_values(stream_key, shape, scale, most, cuts=(), held_as=jnp.bfloat16):
    drawn = scale * jax.random.normal(stream_key, shape, jnp.float32)
    if cuts:
        drawn = drawn * level_of(stream_key, shape, cuts, -0.22, 0.18)
    return jnp.clip(drawn, -most, most).astype(held_as)


def setup_inputs(seed: int = 0) -> dict:
    keys = jax.random.split(jax.random.key(seed), 12)
    queries = draw_queries(jax.random.fold_in(keys[11], 71), 0)
    key_rows = draw_key_rows(jax.random.fold_in(keys[11], 71), 0)
    values = normal_values(keys[2], (SEQUENCE_LENGTH, SEQUENCE_COUNT, KEY_VALUE_HEADS * HEAD_WIDTH), 1.0, 6.0, ((0, 128),))
    hidden = normal_values(keys[3], (SEQUENCE_LENGTH, SEQUENCE_COUNT, D), 1.0, 6.0, ((0, 128),))
    norm_gain = jnp.clip(jnp.exp(jax.random.uniform(keys[4], (D,), jnp.float32, math.log(0.5), math.log(2.0))), 0.5, 2.0)
    routes = choose_distinct(keys[5], SEQUENCE_LENGTH * SEQUENCE_COUNT, EXPERTS, TOPK, 512).reshape((SEQUENCE_LENGTH, SEQUENCE_COUNT, TOPK))
    route_gates = jnp.clip(0.02 + 0.28 * jax.random.uniform(keys[6], (SEQUENCE_LENGTH, SEQUENCE_COUNT, TOPK), jnp.float32) ** level_of(keys[6], (SEQUENCE_LENGTH, SEQUENCE_COUNT, TOPK), ((0, 128),), -0.2, 0.2), 0.02, 0.3)
    expert_home = jax.random.permutation(keys[7], EXPERTS).astype(jnp.int32)
    w_gate = normal_values(keys[8], (EXPERTS, D, FF), D ** -0.5, 0.09375, ((0, 128),))
    w_up = normal_values(keys[9], (EXPERTS, D, FF), D ** -0.5, 0.09375, ((0, 128),))
    w_down = normal_values(keys[10], (EXPERTS, FF, D), FF ** -0.5, 0.21875, ((0, 128),))
    return {"queries": queries, "key_rows": key_rows, "values": values, "hidden": hidden, "norm_gain": norm_gain, "routes": routes, "route_gates": route_gates, "expert_home": expert_home, "w_gate": w_gate, "w_up": w_up, "w_down": w_down}


def attend_sequence(sequence_queries, sequence_keys, sequence_values):
    group_width = QUERY_HEADS // KEY_VALUE_HEADS
    query_block = min(512, SEQUENCE_LENGTH)
    query_groups = sequence_queries.reshape(SEQUENCE_LENGTH, KEY_VALUE_HEADS, group_width, HEAD_WIDTH).astype(jnp.float32)
    widened_keys = sequence_keys.reshape(SEQUENCE_LENGTH, KEY_VALUE_HEADS, HEAD_WIDTH).astype(jnp.float32)
    widened_values = sequence_values.reshape(SEQUENCE_LENGTH, KEY_VALUE_HEADS, HEAD_WIDTH).astype(jnp.float32)
    pieces = []
    for block_index in range(SEQUENCE_LENGTH // query_block):
        first_row = block_index * query_block
        last_row = first_row + query_block
        part_query = query_groups[first_row:last_row]
        scores = jnp.einsum('qhgd,khd->hgqk', part_query, widened_keys[:last_row]) * HEAD_WIDTH ** (-0.5)
        query_pos = first_row + jnp.arange(query_block, dtype=jnp.int32)
        key_pos = jnp.arange(last_row, dtype=jnp.int32)
        visible = key_pos[None, :] <= query_pos[:, None]
        scores = jnp.where(visible, scores, -jnp.inf)
        row_max = lax.optimization_barrier(jnp.max(scores, axis=-1, keepdims=True))
        raised = jnp.exp(scores - row_max)
        row_total = lax.optimization_barrier(jnp.sum(raised, axis=-1, keepdims=True))
        weights = lax.optimization_barrier(raised.astype(jnp.bfloat16)).astype(jnp.float32)
        attended = jnp.einsum('hgqk,khd->qhgd', weights, widened_values[:last_row])
        attended = attended / jnp.transpose(row_total, (2, 0, 1, 3))
        pieces.append(attended.astype(jnp.bfloat16).reshape(query_block, QUERY_HEADS * HEAD_WIDTH))
    return jnp.concatenate(pieces, axis=0)

def reference(queries, key_rows, values, hidden, norm_gain, routes, route_gates, expert_home, w_gate, w_up, w_down):
    context = jnp.stack([attend_sequence(queries[:, seq_index], key_rows[:, seq_index], values[:, seq_index]) for seq_index in range(SEQUENCE_COUNT)], axis=1)
    blocks_all = N_CTX * N_EXP
    token_count = SEQUENCE_LENGTH * SEQUENCE_COUNT
    tokens_flat = hidden.reshape(token_count, D).astype(jnp.float32)
    normed = (tokens_flat * lax.rsqrt(lax.optimization_barrier(jnp.mean(tokens_flat * tokens_flat, axis=-1, keepdims=True)) + 1e-06) * norm_gain).astype(jnp.bfloat16)
    chosen = routes.reshape(blocks_all, TOK_DEV, TOPK)
    picked = (chosen[..., None] == jnp.arange(EXPERTS, dtype=jnp.int32)).astype(jnp.int32)
    per_token = lax.optimization_barrier(jnp.sum(picked, axis=2))
    before = jnp.cumsum(per_token, axis=1) - per_token
    slot_rank = lax.optimization_barrier(jnp.sum(picked * before[:, :, None, :], axis=-1))
    block_id = jnp.arange(blocks_all, dtype=jnp.int32)[:, None, None]
    token_id = block_id * TOK_DEV + jnp.arange(TOK_DEV, dtype=jnp.int32)[None, :, None]
    slot_count = EXPERTS * blocks_all * CAP
    slot_index = (chosen * blocks_all + block_id) * CAP + slot_rank
    slot_index = jnp.where(slot_rank < CAP, slot_index, slot_count).reshape(-1)
    slot_table = jnp.full((slot_count,), token_count, jnp.int32).at[slot_index].set(jnp.broadcast_to(token_id, chosen.shape).reshape(-1), mode='drop')
    gate_table = jnp.zeros((slot_count,), jnp.float32).at[slot_index].set(route_gates.reshape(-1), mode='drop')
    slot_table = slot_table.reshape(EXPERTS, blocks_all * CAP)
    gate_table = gate_table.reshape(EXPERTS, blocks_all * CAP)

    def one_expert(summed, inputs):
        slot_tokens, slot_gates, stored = inputs
        filled = (slot_tokens < token_count).astype(jnp.bfloat16)
        rows_in = normed[jnp.minimum(slot_tokens, token_count - 1)] * filled[:, None]
        gate_proj = jnp.dot(rows_in, w_gate[stored], preferred_element_type=jnp.float32)
        up_proj = jnp.dot(rows_in, w_up[stored], preferred_element_type=jnp.float32)
        active = (jax.nn.silu(gate_proj) * up_proj).astype(jnp.bfloat16)
        expert_out = jnp.dot(active, w_down[stored], preferred_element_type=jnp.float32).astype(jnp.bfloat16)
        summed = summed.at[slot_tokens].add(slot_gates[:, None] * expert_out.astype(jnp.float32), mode='drop')
        return (summed, None)
    summed, unused = lax.scan(one_expert, jnp.zeros((token_count, D), jnp.float32), (slot_table, gate_table, expert_home))
    layer_out = (tokens_flat + summed).astype(jnp.bfloat16).reshape(SEQUENCE_LENGTH, SEQUENCE_COUNT, D)
    return (context, layer_out)
```

```python
import jax
import jax.numpy as jnp
import numpy as np
from jax import lax
from jax.experimental import pallas as pl
from jax.experimental.pallas import tpu as pltpu
from jax.sharding import PartitionSpec as P

MESH = pl.DeviceIdType.MESH
HEAD_WIDTH = 128
TOPK = 8
WIDTH = 4096
FF = 768
CAP = 3
TOKENS = 64
SLOTS = 384
CHUNKS = 8
CHUNK = WIDTH // CHUNKS
BLOCK = 1024
ORDERS = (("y", "z", "w"), ("z", "w", "y"), ("w", "y", "z"))
SIZES = {"y": 4, "z": 4, "w": 8}
AXIS_CODE = {"y": 0, "z": 1, "w": 2}
NEG = -1e30
BF = jnp.bfloat16
F32 = jnp.float32


def slot_tables():
    columns = np.zeros((SLOTS, 128), np.int32)
    rows = np.zeros((3, 16, SLOTS), np.int32)

    def keys_of(axes):
        shape = [SIZES[a] for a in axes] + [CAP]
        grids = np.meshgrid(*[np.arange(n) for n in shape], indexing="ij")
        return {name: grid.reshape(-1) for name, grid in zip(list(axes) + ["r"], grids)}

    def code(keys):
        return ((keys["y"] * 4 + keys["z"]) * 8 + keys["w"]) * CAP + keys["r"]

    def index(new, old):
        where = np.zeros(SLOTS, np.int32)
        where[code(old)] = np.arange(SLOTS)
        return where[code(new)]

    common = keys_of(("w", "z", "y"))
    for o, (a, b, c) in enumerate(ORDERS):
        first, second, third = keys_of((a, b, c)), keys_of((b, a, c)), keys_of((c, b, a))
        table = [
            first["y"], first["z"], first["w"] // 2, first["w"] % 2, first["r"],
            index(second, first), index(third, second), index(common, third),
        ]
        for i, entry in enumerate(table):
            columns[:, o * 8 + i] = entry
            rows[o, i] = entry
    return columns, rows


def kernel(
    q_ref, k_ref, v_ref, hid_ref, gain_ref, routes_ref, gates_ref, home_col_ref, home_row_ref,
    cols_ref, rows_ref, wg_hbm, wu_hbm, wd_hbm,
    ctx_ref, out_ref,
    send, recv, wgu, wd, perm, normed, placing, gating, hidden_acc, active,
    key_own, value_own, keys, values, qd, best, total, acc,
    send_sem, recv_sem, weight_sem, kv_send, kv_recv,
):
    y = lax.axis_index("ctx")
    flat = lax.axis_index("exp")
    z = lax.div(flat, 8)
    w = lax.rem(flat, 8)
    x = lax.div(w, 2)
    c = lax.rem(w, 2)

    def at(dy=0, dz=0, dx=0, dc=0):
        return (
            lax.rem(y + (dy + 4), 4),
            lax.rem(z + (dz + 4), 4) * 8 + lax.rem(x + (dx + 4), 4) * 2 + lax.rem(c + dc, 2),
        )

    barrier = pltpu.get_barrier_semaphore()
    partners = [at(dy=k) for k in (1, 2, 3)] + [at(dz=k) for k in (1, 2, 3)]
    partners += [at(dx=k // 2, dc=k % 2) for k in range(1, 8)]
    for partner in partners:
        pl.semaphore_signal(barrier, inc=1, device_id=partner, device_id_type=MESH)

    def gate_up_copies(j, slot):
        span = pl.ds(pl.multiple_of(j * CHUNK, CHUNK), CHUNK)
        return (
            pltpu.make_async_copy(wg_hbm.at[span], wgu.at[slot, 0], weight_sem.at[slot, 0]),
            pltpu.make_async_copy(wu_hbm.at[span], wgu.at[slot, 1], weight_sem.at[slot, 1]),
        )

    for slot in range(2):
        for copy in gate_up_copies(slot, slot):
            copy.start()
    down_copy = pltpu.make_async_copy(wd_hbm, wd, weight_sem.at[2, 0])
    down_copy.start()

    row64 = lax.broadcasted_iota(jnp.int32, (64, 64), 0)
    col64 = lax.broadcasted_iota(jnp.int32, (64, 64), 1)
    apart64 = (col64 == ((row64 & 31) * 2 + (row64 >> 5))).astype(BF)
    for source, own in ((k_ref, key_own), (v_ref, value_own)):
        parted = jnp.dot(apart64, source[...], preferred_element_type=F32).astype(BF)
        for head in range(2):
            for s in range(2):
                own[head, s] = parted[s * 32:(s + 1) * 32, head * 128:(head + 1) * 128]
    own_head = lax.div(z, 2)
    keys[:, 0, 0, 0, 0] = key_own[own_head]
    values[:, 0, 0, 0, 0] = value_own[own_head]

    pl.semaphore_wait(barrier, len(partners))

    def remote(source, target, step, kind, device):
        return pltpu.make_async_remote_copy(
            src_ref=source, dst_ref=target, send_sem=kv_send.at[step, kind],
            recv_sem=kv_recv.at[step, kind], device_id=device, device_id_type=MESH,
        )

    def kv_first():
        for k in (1, 2, 3):
            head = lax.div(lax.rem(z + k, 4), 2)
            remote(key_own.at[head], keys.at[:, 0, k, 0, 0], 0, 0, at(dz=k)).start()
            remote(value_own.at[head], values.at[:, 0, k, 0, 0], 0, 1, at(dz=k)).start()

    def kv_region(step):
        if step == 0:
            return keys.at[:, 0, pl.ds(1, 3), 0, 0], values.at[:, 0, pl.ds(1, 3), 0, 0]
        if step == 1:
            return keys.at[:, pl.ds(1, 3), :, 0, 0], values.at[:, 0, :, pl.ds(1, 3), 0]
        if step == 2:
            return keys.at[:, :, :, pl.ds(1, 3), 0], values.at[:, pl.ds(1, 3), :, :, 0]
        return keys.at[:, :, :, :, 1], values.at[:, :, :, :, 1]

    def kv_wait(step, sent):
        for kind, region in enumerate(kv_region(step)):
            copy = remote(region, region, step, kind, at(dc=1))
            if sent:
                copy.wait_send()
            else:
                copy.wait_recv()

    def kv_second():
        for k in (2, 1, 3):
            remote(keys.at[:, 0, :, 0, 0], keys.at[:, k, :, 0, 0], 1, 0, at(dy=k)).start()
            remote(values.at[:, 0, :, 0, 0], values.at[:, 0, :, k, 0], 1, 1, at(dx=k)).start()

    def kv_third():
        for k in (2, 1, 3):
            remote(keys.at[:, :, :, 0, 0], keys.at[:, :, :, k, 0], 2, 0, at(dx=k)).start()
            remote(values.at[:, 0, :, :, 0], values.at[:, k, :, :, 0], 2, 1, at(dy=k)).start()

    def kv_fourth():
        remote(keys.at[:, :, :, :, 0], keys.at[:, :, :, :, 1], 3, 0, at(dc=1)).start()
        remote(values.at[:, :, :, :, 0], values.at[:, :, :, :, 1], 3, 1, at(dc=1)).start()

    kv_first()

    tokens = hid_ref[...].astype(F32)
    scale = lax.rsqrt(jnp.mean(tokens * tokens, axis=-1, keepdims=True) + 1e-06)
    for j in range(CHUNKS):
        span = slice(j * CHUNK, (j + 1) * CHUNK)
        part = hid_ref[:, span].astype(F32)
        normed[j] = (part * scale * gain_ref[:, span]).astype(BF)

    expert_lane = lax.broadcasted_iota(jnp.int32, (TOKENS, 128), 1)
    picked = jnp.zeros((TOKENS, 128), F32)
    gate_of = jnp.zeros((TOKENS, 128), F32)
    for k in range(TOPK):
        hit = routes_ref[:, k:k + 1] == expert_lane
        picked = picked + jnp.where(hit, 1.0, 0.0)
        gate_of = gate_of + jnp.where(hit, gates_ref[:, k:k + 1], 0.0)
    earlier = (col64 < row64).astype(BF)
    before = jnp.dot(earlier, picked.astype(BF), preferred_element_type=F32)
    gate_high = gate_of.astype(BF)
    gate_low = (gate_of - gate_high.astype(F32)).astype(BF)
    facts = jnp.concatenate([picked.astype(BF), before.astype(BF), gate_high, gate_low], axis=0)
    for o in range(3):
        def target(field):
            return (
                ((y + field(0)) & 3) * 32 + ((z + field(1)) & 3) * 8
                + ((x + field(2)) & 3) * 2 + ((c + field(3)) & 1)
            )

        dest_col = target(lambda i: cols_ref[:, o * 8 + i:o * 8 + i + 1])
        dest_row = target(lambda i: rows_ref[o, i:i + 1, :])
        hosts_t = (dest_col == home_row_ref[...]).astype(BF)
        hosts = (dest_row == home_col_ref[...]).astype(BF)
        slot_facts_t = lax.dot_general(
            hosts_t, facts[:128], (((1,), (1,)), ((), ())), preferred_element_type=F32
        )
        rank_col = cols_ref[:, o * 8 + 4:o * 8 + 5].astype(F32)
        placing[o] = (
            slot_facts_t[:, :64] * jnp.where(slot_facts_t[:, 64:] == rank_col, 1.0, 0.0)
        ).astype(BF)
        slot_facts = jnp.dot(facts, hosts, preferred_element_type=F32)
        rank_row = rows_ref[o, 4:5, :].astype(F32)
        kept = slot_facts[:64] * jnp.where(slot_facts[64:128] == rank_row, 1.0, 0.0)
        gating[o] = (slot_facts[128:] * jnp.concatenate([kept, kept], axis=0)).astype(BF)

    lane = lax.broadcasted_iota(jnp.int32, (SLOTS, SLOTS), 1)
    sublane = lax.broadcasted_iota(jnp.int32, (SLOTS, SLOTS), 0)
    for o in range(3):
        for i in range(3):
            perm[o * 5 + i] = jnp.where(
                cols_ref[:, o * 8 + 5 + i:o * 8 + 6 + i] == lane, 1.0, 0.0
            ).astype(BF)
        for i in range(2):
            perm[o * 5 + 3 + i] = jnp.where(
                rows_ref[o, 5 + i:6 + i, :] == sublane, 1.0, 0.0
            ).astype(BF)

    def axis_of(o, hop):
        return lax.rem(o + hop, 3)

    def by_axis(axis, four, eight):
        pl.when(axis == 0)(lambda: four(0))
        pl.when(axis == 1)(lambda: four(1))
        pl.when(axis == 2)(eight)

    def piece(stage, j, first, count, device):
        return pltpu.make_async_remote_copy(
            src_ref=send.at[stage % 3, j, pl.ds(first, count)],
            dst_ref=recv.at[stage, j, pl.ds(first, count)],
            send_sem=send_sem.at[stage, j], recv_sem=recv_sem.at[stage, j],
            device_id=device, device_id_type=MESH,
        )

    def start_hop(stage, j, axis):
        sign = 1 if stage < 3 else -1

        def four(which):
            for k in (2, 1, 3):
                device = at(dy=sign * k) if which == 0 else at(dz=sign * k)
                piece(stage, j, 96 * k, 96, device).start()
            recv[stage, j, 0:96] = send[stage % 3, j, 0:96]

        def eight():
            for k in (4, 5, 2, 6, 3, 7, 1):
                piece(stage, j, 48 * k, 48, at(dx=sign * (k // 2), dc=k % 2)).start()
            recv[stage, j, 0:48] = send[stage % 3, j, 0:48]

        by_axis(axis, four, eight)

    def wait_hop(stage, j, axis):
        here = at(dc=1)
        by_axis(
            axis,
            lambda which: piece(stage, j, 96, 288, here).wait_recv(),
            lambda: piece(stage, j, 48, 336, here).wait_recv(),
        )

    def wait_sent(stage, j, axis):
        here = at(dc=1)
        by_axis(
            axis,
            lambda which: piece(stage, j, 96, 288, here).wait_send(),
            lambda: piece(stage, j, 48, 336, here).wait_send(),
        )

    def reorder(stage, j, matrix):
        for half in range(2):
            span = pl.ds(half * (CHUNK // 2), CHUNK // 2)
            send[(stage + 1) % 3, j, :, span] = jnp.dot(
                perm[matrix], recv[stage, j, :, span], preferred_element_type=F32
            ).astype(BF)

    def loop(step):
        def one(j, carry):
            step(j, lax.rem(j, 3))
            return carry

        lax.fori_loop(0, CHUNKS, one, 0)

    kv_wait(0, False)
    kv_second()

    def place_step(j, o):
        send[0, j] = jnp.dot(placing[o], normed[j], preferred_element_type=F32).astype(BF)
        start_hop(0, j, axis_of(o, 0))

    loop(place_step)

    row256 = lax.broadcasted_iota(jnp.int32, (256, 256), 0)
    col256 = lax.broadcasted_iota(jnp.int32, (256, 256), 1)
    apart256 = (col256 == ((row256 & 127) * 2 + (row256 >> 7))).astype(BF)
    for b in range(8):
        parted = jnp.dot(
            apart256, q_ref[b * 256:(b + 1) * 256], preferred_element_type=F32
        ).astype(BF)
        for s in range(2):
            qd[s, b * 128:(b + 1) * 128] = parted[s * 128:(s + 1) * 128]
    best[...] = jnp.full_like(best, NEG)
    total[...] = jnp.zeros_like(total)
    acc[...] = jnp.zeros_like(acc)

    kv_wait(1, False)
    kv_third()

    def second_step(j, o):
        wait_hop(0, j, axis_of(o, 0))
        reorder(0, j, o * 5)
        start_hop(1, j, axis_of(o, 1))

    loop(second_step)

    kv_wait(2, False)
    kv_fourth()

    def third_step(j, o):
        wait_hop(1, j, axis_of(o, 1))
        reorder(1, j, o * 5 + 1)
        start_hop(2, j, axis_of(o, 2))

    loop(third_step)

    hidden_acc[...] = jnp.zeros_like(hidden_acc)

    def project_step(j, o):
        wait_hop(2, j, axis_of(o, 2))
        slot = lax.rem(j, 2)
        for copy in gate_up_copies(j, slot):
            copy.wait()
        rows_in = jnp.dot(perm[o * 5 + 2], recv[2, j], preferred_element_type=F32).astype(BF)
        for which in range(2):
            for part in range(2):
                span = pl.ds(part * 384, 384)
                hidden_acc[which, :, span] += jnp.dot(
                    rows_in, wgu[slot, which, :, span], preferred_element_type=F32
                )

        @pl.when(j + 2 < CHUNKS)
        def _():
            for copy in gate_up_copies(j + 2, slot):
                copy.start()

    loop(project_step)

    gate_proj = hidden_acc[0]
    rows_mid = (gate_proj / (1.0 + jnp.exp(-gate_proj)) * hidden_acc[1]).astype(BF)
    for o in range(3):
        back = jnp.where(rows_ref[o, 7:8, :] == sublane, 1.0, 0.0).astype(BF)
        active[o] = jnp.dot(back, rows_mid, preferred_element_type=F32).astype(BF)
    down_copy.wait()

    def produce_step(j, o):
        wait_sent(0, j, axis_of(o, 0))
        span = pl.ds(pl.multiple_of(j * CHUNK, CHUNK), CHUNK)
        send[0, j] = jnp.dot(active[o], wd[:, span], preferred_element_type=F32).astype(BF)
        start_hop(3, j, axis_of(o, 2))

    loop(produce_step)

    kv_wait(3, False)
    lane_key = lax.broadcasted_iota(jnp.int32, (1, BLOCK), 1)
    key_pos = (
        ((z + 4 - (lane_key >> 8)) & 3) * 256
        + ((x + 4 - ((lane_key >> 6) & 3)) & 3) * 64
        + ((c + (lane_key >> 5)) & 1) * 32
        + (lane_key & 31)
    )
    factor = HEAD_WIDTH ** (-0.5) * 1.4426950408889634

    def attend(t):
        behind = lax.div(t, 4)
        s = lax.rem(lax.div(t, 2), 2)
        half = lax.rem(t, 2)

        @pl.when(behind <= y)
        def _():
            block_keys = keys[s, behind].reshape(BLOCK, HEAD_WIDTH)
            block_values = values[s, behind].reshape(BLOCK, HEAD_WIDTH)
            for q in range(2):
                first = pl.multiple_of(half * 512 + q * 256, 256)
                span = pl.ds(first, 256)
                scores = lax.dot_general(
                    qd[s, span], block_keys, (((1,), (1,)), ((), ())),
                    preferred_element_type=F32,
                ) * factor
                query_pos = lax.broadcasted_iota(jnp.int32, (256, 1), 0) + (
                    first + behind * BLOCK
                )
                scores = jnp.where(key_pos <= query_pos, scores, NEG)
                best_old = best[s, span]
                best_new = jnp.maximum(best_old, jnp.max(scores, axis=-1, keepdims=True))
                weights = jnp.exp2(scores - best_new[:, :1])
                shrink = jnp.exp2(best_old - best_new)
                best[s, span] = best_new
                total[s, span] = total[s, span] * shrink + jnp.sum(
                    weights, axis=-1, keepdims=True
                )
                acc[s, span] = acc[s, span] * shrink + jnp.dot(
                    weights.astype(BF), block_values, preferred_element_type=F32
                )

    def return_second_step(j, o):
        wait_hop(3, j, axis_of(o, 2))
        wait_sent(1, j, axis_of(o, 1))
        reorder(3, j, o * 5 + 4)
        start_hop(4, j, axis_of(o, 1))
        attend(j)

    loop(return_second_step)

    def return_third_step(j, o):
        wait_hop(4, j, axis_of(o, 1))
        wait_sent(2, j, axis_of(o, 2))
        reorder(4, j, o * 5 + 3)
        start_hop(5, j, axis_of(o, 0))
        attend(j + 8)

    loop(return_third_step)

    together = (col256 == ((row256 & 1) * 128 + (row256 >> 1))).astype(BF)
    for b in range(8):
        span = slice(b * 128, (b + 1) * 128)
        both = jnp.concatenate(
            [(acc[s, span] / total[s, span]).astype(BF) for s in range(2)], axis=0
        )
        ctx_ref[b * 256:(b + 1) * 256] = jnp.dot(
            together, both, preferred_element_type=F32
        ).astype(BF)

    def combine_step(j, o):
        wait_hop(5, j, axis_of(o, 0))
        span = pl.ds(pl.multiple_of(j * CHUNK, CHUNK), CHUNK)
        mixed = jnp.dot(gating[o], recv[5, j], preferred_element_type=F32)
        out_ref[:, span] = (
            hid_ref[:, span].astype(F32) + mixed[:64] + mixed[64:]
        ).astype(BF)

    loop(combine_step)

    def drain_step(j, o):
        wait_sent(3, j, axis_of(o, 2))
        wait_sent(4, j, axis_of(o, 1))
        wait_sent(5, j, axis_of(o, 0))

    loop(drain_step)
    for step in range(4):
        kv_wait(step, True)


def body(
    queries, key_rows, values, hidden, norm_gain, routes, route_gates, expert_home,
    w_gate, w_up, w_down,
):
    columns, rows = slot_tables()
    vmem = pl.BlockSpec(memory_space=pltpu.VMEM)
    hbm = pl.BlockSpec(memory_space=pl.ANY)
    block = (CHUNKS, SLOTS, CHUNK)
    context, layer_out = pl.pallas_call(
        kernel,
        out_shape=(
            jax.ShapeDtypeStruct((2 * BLOCK, HEAD_WIDTH), BF),
            jax.ShapeDtypeStruct((TOKENS, WIDTH), BF),
        ),
        in_specs=[vmem] * 11 + [hbm] * 3,
        out_specs=(vmem, vmem),
        scratch_shapes=[
            pltpu.VMEM((3,) + block, BF),
            pltpu.VMEM((6,) + block, BF),
            pltpu.VMEM((2, 2, CHUNK, FF), BF),
            pltpu.VMEM((FF, WIDTH), BF),
            pltpu.VMEM((15, SLOTS, SLOTS), BF),
            pltpu.VMEM((CHUNKS, TOKENS, CHUNK), BF),
            pltpu.VMEM((3, SLOTS, TOKENS), BF),
            pltpu.VMEM((3, 2 * TOKENS, SLOTS), BF),
            pltpu.VMEM((2, SLOTS, FF), F32),
            pltpu.VMEM((3, SLOTS, FF), BF),
            pltpu.VMEM((2, 2, 32, HEAD_WIDTH), BF),
            pltpu.VMEM((2, 2, 32, HEAD_WIDTH), BF),
            pltpu.VMEM((2, 4, 4, 4, 2, 32, HEAD_WIDTH), BF),
            pltpu.VMEM((2, 4, 4, 4, 2, 32, HEAD_WIDTH), BF),
            pltpu.VMEM((2, BLOCK, HEAD_WIDTH), BF),
            pltpu.VMEM((2, BLOCK, HEAD_WIDTH), F32),
            pltpu.VMEM((2, BLOCK, HEAD_WIDTH), F32),
            pltpu.VMEM((2, BLOCK, HEAD_WIDTH), F32),
            pltpu.SemaphoreType.DMA((6, CHUNKS)),
            pltpu.SemaphoreType.DMA((6, CHUNKS)),
            pltpu.SemaphoreType.DMA((3, 2)),
            pltpu.SemaphoreType.DMA((4, 2)),
            pltpu.SemaphoreType.DMA((4, 2)),
        ],
        compiler_params=pltpu.CompilerParams(
            collective_id=0, has_side_effects=True, vmem_limit_bytes=62 * 2**20
        ),
    )(
        queries.reshape(2 * BLOCK, HEAD_WIDTH),
        key_rows.reshape(TOKENS, 2 * HEAD_WIDTH),
        values.reshape(TOKENS, 2 * HEAD_WIDTH),
        hidden.reshape(TOKENS, WIDTH),
        norm_gain.reshape(1, WIDTH),
        routes.reshape(TOKENS, TOPK),
        route_gates.reshape(TOKENS, TOPK),
        expert_home.reshape(128, 1),
        expert_home.reshape(1, 128),
        jnp.asarray(columns),
        jnp.asarray(rows),
        w_gate[0],
        w_up[0],
        w_down[0],
    )
    return context.reshape(queries.shape), layer_out.reshape(hidden.shape)


def solution(mesh):
    both = P(("ctx", "exp"), None, None)
    in_specs = (P("ctx", None, "exp"), both, both, both, P(), both, both, P(), both, both, both)
    out_specs = (P("ctx", None, "exp"), both)
    return jax.shard_map(body, mesh=mesh, in_specs=in_specs, out_specs=out_specs, check_vma=False)
```

```python
import jax
import jax.numpy as jnp
import numpy as np
from jax import lax
from jax.experimental import pallas as pl
from jax.experimental.pallas import tpu as pltpu
from jax.sharding import PartitionSpec as P

MESH = pl.DeviceIdType.MESH
HEAD_WIDTH = 128
TOPK = 8
WIDTH = 4096
FF = 768
CAP = 3
TOKENS = 64
SLOTS = 384
CHUNKS = 8
CHUNK = WIDTH // CHUNKS
BLOCK = 1024
ORDERS = (("y", "z", "x"), ("z", "x", "y"), ("x", "y", "z"))
NEG = -1e30
BF = jnp.bfloat16
F32 = jnp.float32


def slot_tables():
    grids = np.indices((4, 4, 8, CAP)).reshape(4, SLOTS)

    def index(new, old, sizes):
        where = np.zeros(SLOTS, np.int32)
        where[np.ravel_multi_index(old, sizes)] = np.arange(SLOTS)
        return where[np.ravel_multi_index(new, sizes)]

    by_start = list(grids)
    by_middle = np.indices((4, 4, 8, CAP)).reshape(4, SLOTS)[[1, 0, 2, 3]]
    by_end = np.indices((8, 4, 4, CAP)).reshape(4, SLOTS)[[2, 1, 0, 3]]
    sizes = (4, 4, 8, CAP)
    columns = np.zeros((SLOTS, 128), np.int32)
    rows = np.zeros((8, SLOTS), np.int32)
    columns[:, 0] = index(by_middle, by_start, sizes)
    columns[:, 1] = index(by_end, by_middle, sizes)
    rows[0] = columns[:, 1]

    def offsets(keys, axes):
        found = dict(zip(axes, (keys[0], keys[1], keys[2] // 2)))
        return [found["y"], found["z"], found["x"], keys[2] % 2, keys[3]]

    common = offsets(by_end, ORDERS[0])
    for o, axes in enumerate(ORDERS):
        for i, entry in enumerate(offsets(by_start, axes)):
            columns[:, 8 + o * 8 + i] = entry
        rows[1 + o] = index(common, offsets(by_end, axes), (4, 4, 4, 2, CAP))
        columns[:, 2 + o] = rows[1 + o]
    return columns, rows


def kernel(
    q_ref, k_ref, v_ref, hid_ref, gain_ref, routes_ref, gates_ref, home_ref,
    cols_ref, rows_ref, wg_hbm, wu_hbm, wd_hbm,
    ctx_ref, out_ref,
    send, recv, recv_first, recv_last, wgu, wd, perm, normed, gates_own, gates_all, placing,
    gating, hidden_acc, rows_in, active,
    key_own, value_own, keys, values, qd, best, total, acc,
    send_sem, recv_sem, gate_send, gate_recv, weight_sem, kv_send, kv_recv,
):
    y = lax.axis_index("ctx")
    flat = lax.axis_index("exp")
    z = lax.div(flat, 8)
    w = lax.rem(flat, 8)
    x = lax.div(w, 2)
    c = lax.rem(w, 2)

    def at(dy=0, dz=0, dx=0, dc=0):
        return (
            lax.rem(y + (dy + 4), 4),
            lax.rem(z + (dz + 4), 4) * 8 + lax.rem(x + (dx + 4), 4) * 2 + lax.rem(c + dc, 2),
        )

    barrier = pltpu.get_barrier_semaphore()
    partners = [at(dc=1)]
    for axis in ("dy", "dz", "dx"):
        partners += [at(**{axis: k, "dc": n}) for k in (1, 2, 3) for n in (0, 1)]
    for partner in partners:
        pl.semaphore_signal(barrier, inc=1, device_id=partner, device_id_type=MESH)

    def gate_up_copies(j, slot):
        span = pl.ds(pl.multiple_of(j * CHUNK, CHUNK), CHUNK)
        return (
            pltpu.make_async_copy(wg_hbm.at[span], wgu.at[slot, 0], weight_sem.at[slot, 0]),
            pltpu.make_async_copy(wu_hbm.at[span], wgu.at[slot, 1], weight_sem.at[slot, 1]),
        )

    for slot in range(2):
        for copy in gate_up_copies(slot, slot):
            copy.start()
    down_copy = pltpu.make_async_copy(wd_hbm, wd, weight_sem.at[2, 0])
    down_copy.start()

    row256 = lax.broadcasted_iota(jnp.int32, (256, 256), 0)
    col256 = lax.broadcasted_iota(jnp.int32, (256, 256), 1)
    apart_tiles = (
        col256 == (row256 & 3) * 64 + (row256 >> 3) * 2 + ((row256 >> 2) & 1)
    ).astype(BF)
    for b in range(8):
        parted = jnp.dot(
            apart_tiles, hid_ref[b * 256:(b + 1) * 256], preferred_element_type=F32
        )
        for tile in range(32):
            out_ref[b * 8:(b + 1) * 8, tile * 128:(tile + 1) * 128] = (
                parted[tile * 8:(tile + 1) * 8]
            )

    tokens = out_ref[...]
    scale = lax.rsqrt(jnp.mean(tokens * tokens, axis=-1, keepdims=True) + 1e-06)
    for j in range(CHUNKS):
        span = slice(j * CHUNK, (j + 1) * CHUNK)
        normed[j] = (out_ref[:, span] * scale * gain_ref[:, span]).astype(BF)

    row128 = lax.broadcasted_iota(jnp.int32, (128, 128), 0)
    col128 = lax.broadcasted_iota(jnp.int32, (128, 128), 1)
    apart128 = (
        col128 == (row128 & 31) * 4 + (row128 >> 6) * 2 + ((row128 >> 5) & 1)
    ).astype(BF)
    for source, own in ((k_ref, key_own), (v_ref, value_own)):
        parted = jnp.dot(apart128, source[...], preferred_element_type=F32).astype(BF)
        for head in range(2):
            for s in range(2):
                first = head * 64 + s * 32
                own[head, s] = parted[first:first + 32]
    own_head = lax.div(z, 2)
    keys[:, 0, 0, 0, 0] = key_own[own_head]
    values[:, 0, 0, 0, 0] = value_own[own_head]

    def remote(source, target, step, kind, n, device):
        return pltpu.make_async_remote_copy(
            src_ref=source, dst_ref=target, send_sem=kv_send.at[step, kind, n],
            recv_sem=kv_recv.at[step, kind, n], device_id=device, device_id_type=MESH,
        )

    def kv_first():
        for k in (1, 2, 3):
            head = lax.div(lax.rem(z + k, 4), 2)
            remote(key_own.at[head], keys.at[:, 0, k, 0, 0], 0, 0, 0, at(dz=k)).start()
            remote(value_own.at[head], values.at[:, 0, k, 0, 0], 0, 1, 0, at(dz=k)).start()

    def kv_second():
        for k in (2, 1, 3):
            @pl.when(y + k < 4)
            def _():
                remote(keys.at[:, 0, :, 0, 0], keys.at[:, k, :, 0, 0], 1, 0, k, at(dy=k)).start()

            remote(values.at[:, 0, :, 0, 0], values.at[:, 0, :, k, 0], 1, 1, 0, at(dx=k)).start()

    def kv_third():
        for k in (2, 1, 3):
            @pl.when(y + k < 4)
            def _():
                remote(values.at[:, 0, :, :, 0], values.at[:, k, :, :, 0], 2, 1, k, at(dy=k)).start()

        for n in range(4):
            @pl.when(n <= y)
            def _():
                for k in (2, 1, 3):
                    remote(keys.at[:, n, :, 0, 0], keys.at[:, n, :, k, 0], 2, 0, n, at(dx=k)).start()

    def kv_fourth():
        for n in range(4):
            @pl.when(n <= y)
            def _():
                remote(keys.at[:, n, :, :, 0], keys.at[:, n, :, :, 1], 3, 0, n, at(dc=1)).start()
                remote(values.at[:, n, :, :, 0], values.at[:, n, :, :, 1], 3, 1, n, at(dc=1)).start()

    def kv_wait(step, sent):
        def wait(region, kind, n):
            copy = remote(region, region, step, kind, n, at(dc=1))
            if sent:
                copy.wait_send()
            else:
                copy.wait_recv()

        if step == 0:
            wait(keys.at[:, 0, pl.ds(1, 3), 0, 0], 0, 0)
            wait(values.at[:, 0, pl.ds(1, 3), 0, 0], 1, 0)
        if step == 1:
            wait(values.at[:, 0, :, pl.ds(1, 3), 0], 1, 0)
        for n in range(4):
            if step in (1, 2) and n > 0:
                @pl.when(y + n < 4 if sent else n <= y)
                def _():
                    if step == 1:
                        wait(keys.at[:, n, :, 0, 0], 0, n)
                    else:
                        wait(values.at[:, n, :, :, 0], 1, n)

            if step in (2, 3):
                @pl.when(n <= y)
                def _():
                    if step == 2:
                        wait(keys.at[:, n, :, pl.ds(1, 3), 0], 0, n)
                    else:
                        wait(keys.at[:, n, :, :, 1], 0, n)
                        wait(values.at[:, n, :, :, 1], 1, n)

    def sources(stage, j):
        if stage == 0:
            return None, recv_first.at[j]
        if stage == 5:
            return send.at[0, j], recv_last.at[j]
        return send.at[(stage + 1) % 2, j], recv.at[stage - 1, j]

    group_rows = (64, 96, 48, 48, 96, 64)

    def piece(stage, j, group, groups, device):
        source, target = sources(stage, j)
        span = pl.ds(group * group_rows[stage], groups * group_rows[stage])
        if stage == 0:
            source = normed.at[j] if groups == 1 else target.at[span]
        else:
            source = source.at[span]
        return pltpu.make_async_remote_copy(
            src_ref=source, dst_ref=target.at[span],
            send_sem=send_sem.at[stage, j], recv_sem=recv_sem.at[stage, j],
            device_id=device, device_id_type=MESH,
        )

    def along(o, hop, act):
        for n, axes in enumerate(ORDERS):
            pl.when(o == n)(lambda axis="d" + axes[hop]: act(axis))

    def start_hop(stage, j, o):
        hop = stage if stage < 3 else 5 - stage
        sign = 1 if stage < 3 else -1

        def start(axis):
            if hop == 2:
                for k in (4, 5, 2, 6, 3, 7, 1):
                    device = at(**{axis: sign * (k // 2), "dc": k % 2})
                    piece(stage, j, k, 1, device).start()
            else:
                for k in (2, 1, 3):
                    piece(stage, j, k, 1, at(**{axis: sign * k})).start()

        along(o, hop, start)
        rows = group_rows[stage]
        source, target = sources(stage, j)
        if stage == 0:
            target[0:rows] = normed[j]
        else:
            target[0:rows] = source[0:rows]

    def wait_hop(stage, j):
        piece(stage, j, 1, 7 if stage in (2, 3) else 3, at(dc=1)).wait_recv()

    def wait_sent(stage, j):
        piece(stage, j, 1, 7 if stage in (2, 3) else 3, at(dc=1)).wait_send()

    def loop(step, first=0, last=CHUNKS):
        def one(j, carry):
            step(j)
            return carry

        lax.fori_loop(first, last, one, 0)

    def order(j):
        return lax.rem(j, 3)

    pl.semaphore_wait(barrier, len(partners))


    kv_first()
    loop(lambda j: start_hop(0, j, order(j)), 0, 4)

    expert_row = lax.broadcasted_iota(jnp.int32, (128, 32), 0)
    picked_parts, gate_parts = [], []
    for s in range(2):
        picked = jnp.zeros((128, 32), F32)
        gate_of = jnp.zeros((128, 32), F32)
        for k in range(TOPK):
            n = s * TOPK + k
            hit = routes_ref[n:n + 1, :] == expert_row
            picked = picked + jnp.where(hit, 1.0, 0.0)
            gate_of = gate_of + jnp.where(hit, gates_ref[n:n + 1, :], 0.0)
        picked_parts.append(picked)
        gate_parts.append(gate_of)
    picked = jnp.concatenate(picked_parts, axis=1)
    gate_of = jnp.concatenate(gate_parts, axis=1)
    row64 = lax.broadcasted_iota(jnp.int32, (64, 64), 0)
    col64 = lax.broadcasted_iota(jnp.int32, (64, 64), 1)
    position = (col64 >> 3) * 4 + (col64 & 3)
    sequence = (col64 >> 2) & 1
    in_order = (row64 == sequence * 32 + position).astype(BF)
    earlier = ((row64 & 31) * 2 + (row64 >> 5) < position * 2 + sequence).astype(BF)
    gate_high = gate_of.astype(BF)
    gate_low = (gate_of - gate_high.astype(F32)).astype(BF)
    facts = [
        jnp.dot(part, matrix, preferred_element_type=F32).astype(BF)
        for part, matrix in (
            (picked.astype(BF), in_order), (picked.astype(BF), earlier),
            (gate_high, in_order), (gate_low, in_order),
        )
    ]
    def gate_copy(o, group, groups, device):
        span = pl.ds(96 * group, 96 * groups)
        return pltpu.make_async_remote_copy(
            src_ref=gates_own.at[o, span], dst_ref=gates_all.at[o, span],
            send_sem=gate_send.at[o], recv_sem=gate_recv.at[o],
            device_id=device, device_id_type=MESH,
        )

    for o in range(3):
        def target(field):
            return (
                ((y + field(0)) & 3) * 32 + ((z + field(1)) & 3) * 8
                + ((x + field(2)) & 3) * 2 + ((c + field(3)) & 1)
            )

        dest = target(lambda i: cols_ref[:, 8 + o * 8 + i:9 + o * 8 + i])
        hosts = (dest == home_ref[...]).astype(BF)
        named, rank, high, low = [
            jnp.dot(hosts, fact, preferred_element_type=F32) for fact in facts
        ]
        kept = named * jnp.where(
            rank == cols_ref[:, 12 + o * 8:13 + o * 8].astype(F32), 1.0, 0.0
        )
        gates_own[o] = jnp.concatenate([high * kept, low * kept], axis=1).astype(BF)
        gates_all[o, 0:96] = gates_own[o, 0:96]
        for k in (1, 2, 3):
            gate_copy(o, k, 1, at(**{"d" + ORDERS[o][0]: k})).start()

    loop(lambda j: start_hop(0, j, order(j)), 4, 8)
    kv_wait(0, False)
    kv_second()

    lane = lax.broadcasted_iota(jnp.int32, (SLOTS, SLOTS), 1)
    sublane = lax.broadcasted_iota(jnp.int32, (SLOTS, SLOTS), 0)
    for i in (0, 1, 3, 4):
        perm[i] = jnp.where(cols_ref[:, i:i + 1] == lane, 1.0, 0.0).astype(BF)
    perm[2] = jnp.where(rows_ref[0:1, :] == sublane, 1.0, 0.0).astype(BF)

    def reorder(stage, j, matrix):
        for half in range(2):
            span = pl.ds(half * (CHUNK // 2), CHUNK // 2)
            send[stage % 2, j, :, span] = jnp.dot(
                perm[matrix], recv[stage - 1, j, :, span], preferred_element_type=F32
            ).astype(BF)

    own_group = (
        lax.broadcasted_iota(jnp.int32, (SLOTS, 256), 1) >> 6
        == lax.div(lax.broadcasted_iota(jnp.int32, (SLOTS, 256), 0), 96)
    )
    for o in range(3):
        gate_copy(o, 1, 3, at(dc=1)).wait_recv()
        high = gates_all[o, :, 0:64].astype(F32)
        filled = jnp.where(
            jnp.logical_and(own_group, jnp.concatenate([high] * 4, axis=1) != 0.0), 1.0, 0.0
        ).astype(BF)
        placing[o] = jnp.dot(perm[0], filled, preferred_element_type=F32).astype(BF)

    def build_gating():
        for o in range(3):
            for n in range(2):
                part = gates_all[o, :, n * 64:(n + 1) * 64].astype(F32)
                spread = jnp.where(own_group, jnp.concatenate([part] * 4, axis=1), 0.0)
                gating[o, n * 256:(n + 1) * 256] = jnp.transpose(
                    jnp.dot(perm[0], spread.astype(BF), preferred_element_type=F32)
                ).astype(BF)

    def second_step(j):
        o = order(j)
        wait_hop(0, j)
        for half in range(2):
            span = pl.ds(half * (CHUNK // 2), CHUNK // 2)
            send[0, j, :, span] = jnp.dot(
                placing[o], recv_first[j, :, span], preferred_element_type=F32
            ).astype(BF)
        start_hop(1, j, o)

    def third_step(j):
        o = order(j)
        wait_hop(1, j)
        reorder(1, j, 1)
        start_hop(2, j, o)

    def project_step(j):
        o = order(j)
        wait_hop(2, j)
        slot = lax.rem(j, 2)
        for copy in gate_up_copies(j, slot):
            copy.wait()

        @pl.when(o == 0)
        def _():
            rows_in[...] = recv[1, j]

        @pl.when(o > 0)
        def _():
            rows_in[...] = jnp.dot(
                perm[o + 2], recv[1, j], preferred_element_type=F32
            ).astype(BF)

        for which in range(2):
            for part in range(2):
                span = pl.ds(part * 384, 384)
                hidden_acc[which, :, span] += jnp.dot(
                    rows_in[...], wgu[slot, which, :, span], preferred_element_type=F32
                )

        @pl.when(j + 2 < CHUNKS)
        def _():
            for copy in gate_up_copies(j + 2, slot):
                copy.start()

    loop(second_step, 0, 4)

    apart256 = (col256 == ((row256 & 127) * 2 + (row256 >> 7))).astype(BF)
    for b in range(8):
        parted = jnp.dot(
            apart256, q_ref[b * 256:(b + 1) * 256], preferred_element_type=F32
        ).astype(BF)
        for s in range(2):
            qd[s, b * 128:(b + 1) * 128] = parted[s * 128:(s + 1) * 128]
    best[...] = jnp.full_like(best, NEG)
    total[...] = jnp.zeros_like(total)
    acc[...] = jnp.zeros_like(acc)

    hidden_acc[...] = jnp.zeros_like(hidden_acc)
    build_gating()

    def second_third(j):
        second_step(j)
        third_step(j - 4)

    def third_project(j):
        third_step(j)
        project_step(j - 4)

    loop(second_third, 4, 8)
    loop(third_project, 4, 8)
    kv_wait(1, False)
    kv_third()
    loop(project_step, 4, 8)

    gate_proj = hidden_acc[0]
    active[0] = (gate_proj / (1.0 + jnp.exp(-gate_proj)) * hidden_acc[1]).astype(BF)
    down_copy.wait()

    def produce_step(j):
        o = order(j)
        @pl.when(jnp.logical_and(j > 0, j < 3))
        def _():
            back = jnp.where(rows_ref[pl.ds(o + 1, 1), :] == sublane, 1.0, 0.0).astype(BF)
            active[o] = jnp.dot(back, active[0], preferred_element_type=F32).astype(BF)

        wait_sent(1, j)
        span = pl.ds(pl.multiple_of(j * CHUNK, CHUNK), CHUNK)
        send[0, j] = jnp.dot(active[o], wd[:, span], preferred_element_type=F32).astype(BF)
        start_hop(3, j, o)

    loop(produce_step)

    lane_key = lax.broadcasted_iota(jnp.int32, (1, BLOCK), 1)
    key_pos = (
        ((z + 4 - (lane_key >> 8)) & 3) * 256
        + ((x + 4 - ((lane_key >> 6) & 3)) & 3) * 64
        + ((c + (lane_key >> 5)) & 1) * 32
        + (lane_key & 31)
    )
    factor = HEAD_WIDTH ** (-0.5) * 1.4426950408889634

    def attend(t):
        behind = lax.div(t, 4)
        s = lax.rem(lax.div(t, 2), 2)
        half = lax.rem(t, 2)

        def block(masked):
            block_keys = keys[s, behind].reshape(BLOCK, HEAD_WIDTH)
            block_values = values[s, behind].reshape(BLOCK, HEAD_WIDTH)
            for q in range(2):
                first = pl.multiple_of(half * 512 + q * 256, 256)
                span = pl.ds(first, 256)
                scores = lax.dot_general(
                    qd[s, span], block_keys, (((1,), (1,)), ((), ())),
                    preferred_element_type=F32,
                ) * factor
                if masked:
                    query_pos = lax.broadcasted_iota(jnp.int32, (256, 1), 0) + first
                    scores = jnp.where(key_pos <= query_pos, scores, NEG)
                best_old = best[s, span]
                best_new = jnp.maximum(best_old, jnp.max(scores, axis=-1, keepdims=True))
                weights = jnp.exp2(scores - best_new[:, :1])
                shrink = jnp.exp2(best_old - best_new)
                best[s, span] = best_new
                total[s, span] = total[s, span] * shrink + jnp.sum(
                    weights, axis=-1, keepdims=True
                )
                acc[s, span] = acc[s, span] * shrink + jnp.dot(
                    weights.astype(BF), block_values, preferred_element_type=F32
                )

        pl.when(behind == 0)(lambda: block(True))
        pl.when(jnp.logical_and(behind > 0, behind <= y))(lambda: block(False))

    def return_second_step(j):
        wait_hop(3, j)
        wait_sent(2, j)
        reorder(3, j, 2)
        start_hop(4, j, order(j))

        @pl.when(j == 1)
        def _():
            kv_wait(2, False)
            kv_fourth()

        @pl.when(j == 3)
        def _():
            kv_wait(3, False)

        @pl.when(j >= 4)
        def _():
            attend(j - 4)

    loop(return_second_step)

    def return_third_step(j):
        wait_hop(4, j)
        wait_sent(3, j)
        o = order(j)
        for half in range(2):
            span = pl.ds(half * (CHUNK // 2), CHUNK // 2)
            mixed = jnp.dot(gating[o], recv[3, j, :, span], preferred_element_type=F32)
            send[0, j, 0:256, span] = (mixed[:256] + mixed[256:]).astype(BF)
        start_hop(5, j, o)
        attend(j + 4)

    loop(return_third_step)

    def combine_step(j):
        wait_hop(5, j)
        span = pl.ds(pl.multiple_of(j * CHUNK, CHUNK), CHUNK)
        parts = [recv_last[j, k * 64:(k + 1) * 64].astype(F32) for k in range(4)]
        out_ref[:, span] += (parts[0] + parts[1]) + (parts[2] + parts[3])

        @pl.when(j < 4)
        def _():
            attend(j + 12)

    loop(combine_step)

    for s in range(2):
        for b in range(4):
            span = slice(b * 256, (b + 1) * 256)
            ctx_ref[s, span] = (acc[s, span] / total[s, span]).astype(BF)

    def drain_step(j):
        wait_sent(0, j)
        wait_sent(4, j)
        wait_sent(5, j)

    loop(drain_step)
    for o in range(3):
        gate_copy(o, 1, 3, at(dc=1)).wait_send()
    for step in range(4):
        kv_wait(step, True)


def tile_rows(array):
    parts = array.reshape(array.shape[0], 2, -1, 128).transpose(0, 2, 1, 3)
    return parts.reshape(-1, 128)


def finish_kernel(parted_ref, tokens_ref, ctx_ref, out_ref):
    row = lax.broadcasted_iota(jnp.int32, (256, 256), 0)
    col = lax.broadcasted_iota(jnp.int32, (256, 256), 1)
    together = (col == ((row & 1) * 128 + (row >> 1))).astype(BF)
    for b in range(8):
        span = slice(b * 128, (b + 1) * 128)
        both = jnp.concatenate([parted_ref[s, span] for s in range(2)], axis=0)
        ctx_ref[b * 256:(b + 1) * 256] = jnp.dot(
            together, both, preferred_element_type=F32
        ).astype(BF)
    tiles = (col == ((row & 63) >> 1) * 8 + (row & 1) * 4 + (row >> 6)).astype(BF)
    for b in range(8):
        block = jnp.concatenate(
            [tokens_ref[b * 8:(b + 1) * 8, n * 128:(n + 1) * 128] for n in range(32)], axis=0
        ).astype(BF)
        out_ref[b * 256:(b + 1) * 256] = jnp.dot(
            tiles, block, preferred_element_type=F32
        ).astype(BF)


def body(
    queries, key_rows, values, hidden, norm_gain, routes, route_gates, expert_home,
    w_gate, w_up, w_down,
):
    columns, rows = slot_tables()
    vmem = pl.BlockSpec(memory_space=pltpu.VMEM)
    hbm = pl.BlockSpec(memory_space=pl.ANY)
    block = (CHUNKS, SLOTS, CHUNK)
    parted, tokens = pl.pallas_call(
        kernel,
        out_shape=(
            jax.ShapeDtypeStruct((2, BLOCK, HEAD_WIDTH), BF),
            jax.ShapeDtypeStruct((TOKENS, WIDTH), F32),
        ),
        in_specs=[vmem] * 10 + [hbm] * 3,
        out_specs=(vmem, vmem),
        scratch_shapes=[
            pltpu.VMEM((2,) + block, BF),
            pltpu.VMEM((4,) + block, BF),
            pltpu.VMEM((CHUNKS, 4 * TOKENS, CHUNK), BF),
            pltpu.VMEM((CHUNKS, 4 * TOKENS, CHUNK), BF),
            pltpu.VMEM((2, 2, CHUNK, FF), BF),
            pltpu.VMEM((FF, WIDTH), BF),
            pltpu.VMEM((5, SLOTS, SLOTS), BF),
            pltpu.VMEM((CHUNKS, TOKENS, CHUNK), BF),
            pltpu.VMEM((3, SLOTS, 2 * TOKENS), BF),
            pltpu.VMEM((3, SLOTS, 2 * TOKENS), BF),
            pltpu.VMEM((3, SLOTS, 4 * TOKENS), BF),
            pltpu.VMEM((3, 8 * TOKENS, SLOTS), BF),
            pltpu.VMEM((2, SLOTS, FF), F32),
            pltpu.VMEM((SLOTS, CHUNK), BF),
            pltpu.VMEM((3, SLOTS, FF), BF),
            pltpu.VMEM((2, 2, 32, HEAD_WIDTH), BF),
            pltpu.VMEM((2, 2, 32, HEAD_WIDTH), BF),
            pltpu.VMEM((2, 4, 4, 4, 2, 32, HEAD_WIDTH), BF),
            pltpu.VMEM((2, 4, 4, 4, 2, 32, HEAD_WIDTH), BF),
            pltpu.VMEM((2, BLOCK, HEAD_WIDTH), BF),
            pltpu.VMEM((2, BLOCK, HEAD_WIDTH), F32),
            pltpu.VMEM((2, BLOCK, HEAD_WIDTH), F32),
            pltpu.VMEM((2, BLOCK, HEAD_WIDTH), F32),
            pltpu.SemaphoreType.DMA((6, CHUNKS)),
            pltpu.SemaphoreType.DMA((6, CHUNKS)),
            pltpu.SemaphoreType.DMA((3,)),
            pltpu.SemaphoreType.DMA((3,)),
            pltpu.SemaphoreType.DMA((3, 2)),
            pltpu.SemaphoreType.DMA((4, 2, 4)),
            pltpu.SemaphoreType.DMA((4, 2, 4)),
        ],
        compiler_params=pltpu.CompilerParams(
            collective_id=0, has_side_effects=True, vmem_limit_bytes=62 * 2**20
        ),
    )(
        queries.reshape(2 * BLOCK, HEAD_WIDTH),
        tile_rows(key_rows),
        tile_rows(values),
        tile_rows(hidden),
        norm_gain.reshape(1, WIDTH),
        routes.transpose(1, 2, 0).reshape(2 * TOPK, -1),
        route_gates.transpose(1, 2, 0).reshape(2 * TOPK, -1),
        expert_home.reshape(1, 128),
        jnp.asarray(columns),
        jnp.asarray(rows),
        w_gate[0],
        w_up[0],
        w_down[0],
    )
    context, layer_out = pl.pallas_call(
        finish_kernel,
        out_shape=(
            jax.ShapeDtypeStruct((2 * BLOCK, HEAD_WIDTH), BF),
            jax.ShapeDtypeStruct((TOKENS * WIDTH // 128, 128), BF),
        ),
        in_specs=[vmem, vmem],
        out_specs=(vmem, vmem),
    )(parted, tokens)
    layer_out = layer_out.reshape(-1, WIDTH // 128, 2, 128).transpose(0, 2, 1, 3)
    return context.reshape(queries.shape), layer_out.reshape(hidden.shape)


def solution(mesh):
    both = P(("ctx", "exp"), None, None)
    in_specs = (P("ctx", None, "exp"), both, both, both, P(), both, both, P(), both, both, both)
    out_specs = (P("ctx", None, "exp"), both)
    return jax.shard_map(body, mesh=mesh, in_specs=in_specs, out_specs=out_specs, check_vma=False)
```

```python
import jax
import jax.numpy as jnp
import numpy as np
from jax import lax
from jax.experimental import pallas as pl
from jax.experimental.pallas import tpu as pltpu
from jax.sharding import PartitionSpec as P

MESH = pl.DeviceIdType.MESH
HEAD_WIDTH = 128
TOPK = 8
WIDTH = 4096
FF = 768
CAP = 3
TOKENS = 64
SLOTS = 384
CHUNKS = 16
CHUNK = WIDTH // CHUNKS
BLOCK = 1024
ORDERS = (("y", "z", "x"), ("z", "x", "y"), ("x", "y", "z"))
NEG = -1e30
BF = jnp.bfloat16
F32 = jnp.float32


def slot_tables():
    grids = np.indices((4, 4, 8, CAP)).reshape(4, SLOTS)

    def index(new, old, sizes):
        where = np.zeros(SLOTS, np.int32)
        where[np.ravel_multi_index(old, sizes)] = np.arange(SLOTS)
        return where[np.ravel_multi_index(new, sizes)]

    by_start = list(grids)
    by_middle = np.indices((4, 4, 8, CAP)).reshape(4, SLOTS)[[1, 0, 2, 3]]
    by_end = np.indices((8, 4, 4, CAP)).reshape(4, SLOTS)[[2, 1, 0, 3]]
    sizes = (4, 4, 8, CAP)
    columns = np.zeros((SLOTS, 128), np.int32)
    rows = np.zeros((8, SLOTS), np.int32)
    columns[:, 0] = index(by_middle, by_start, sizes)
    columns[:, 1] = index(by_end, by_middle, sizes)
    rows[0] = columns[:, 1]

    def offsets(keys, axes):
        found = dict(zip(axes, (keys[0], keys[1], keys[2] // 2)))
        return [found["y"], found["z"], found["x"], keys[2] % 2, keys[3]]

    common = offsets(by_end, ORDERS[0])
    for o, axes in enumerate(ORDERS):
        for i, entry in enumerate(offsets(by_start, axes)):
            columns[:, 8 + o * 8 + i] = entry
        rows[1 + o] = index(common, offsets(by_end, axes), (4, 4, 4, 2, CAP))
        columns[:, 2 + o] = rows[1 + o]
    return columns, rows


def kernel(
    q_ref, k_ref, v_ref, hid_ref, gain_ref, routes_ref, gates_ref, home_ref,
    cols_ref, rows_ref, wg_hbm, wu_hbm, wd_hbm,
    ctx_ref, out_ref,
    send, recv, recv_first, recv_last, wgu, wd, perm, normed, gates_own, gates_all, placing,
    gating, hidden_acc, rows_in, active,
    key_own, value_own, keys, values, qd,
    send_sem, recv_sem, gate_send, gate_recv, weight_sem, kv_send, kv_recv,
):
    y = lax.axis_index("ctx")
    flat = lax.axis_index("exp")
    z = lax.div(flat, 8)
    w = lax.rem(flat, 8)
    x = lax.div(w, 2)
    c = lax.rem(w, 2)

    def at(dy=0, dz=0, dx=0, dc=0):
        return (
            lax.rem(y + (dy + 4), 4),
            lax.rem(z + (dz + 4), 4) * 8 + lax.rem(x + (dx + 4), 4) * 2 + lax.rem(c + dc, 2),
        )

    barrier = pltpu.get_barrier_semaphore()
    partners = [at(dc=1)]
    for axis in ("dy", "dz", "dx"):
        partners += [at(**{axis: k, "dc": n}) for k in (1, 2, 3) for n in (0, 1)]
    for partner in partners:
        pl.semaphore_signal(barrier, inc=1, device_id=partner, device_id_type=MESH)

    def gate_up_copies(j, slot):
        span = pl.ds(pl.multiple_of(j * CHUNK, CHUNK), CHUNK)
        return (
            pltpu.make_async_copy(wg_hbm.at[span], wgu.at[slot, 0], weight_sem.at[slot, 0]),
            pltpu.make_async_copy(wu_hbm.at[span], wgu.at[slot, 1], weight_sem.at[slot, 1]),
        )

    for slot in range(2):
        for copy in gate_up_copies(slot, slot):
            copy.start()
    down_copy = pltpu.make_async_copy(wd_hbm, wd, weight_sem.at[2, 0])
    down_copy.start()

    row256 = lax.broadcasted_iota(jnp.int32, (256, 256), 0)
    col256 = lax.broadcasted_iota(jnp.int32, (256, 256), 1)
    apart_tiles = (
        col256 == (row256 & 3) * 64 + (row256 >> 3) * 2 + ((row256 >> 2) & 1)
    ).astype(BF)
    for b in range(8):
        parted = jnp.dot(
            apart_tiles, hid_ref[b * 256:(b + 1) * 256], preferred_element_type=F32
        )
        for tile in range(32):
            out_ref[b * 8:(b + 1) * 8, tile * 128:(tile + 1) * 128] = (
                parted[tile * 8:(tile + 1) * 8]
            )

    tokens = out_ref[...]
    scale = lax.rsqrt(jnp.mean(tokens * tokens, axis=-1, keepdims=True) + 1e-06)
    for j in range(CHUNKS):
        span = slice(j * CHUNK, (j + 1) * CHUNK)
        normed[j] = (out_ref[:, span] * scale * gain_ref[:, span]).astype(BF)

    row128 = lax.broadcasted_iota(jnp.int32, (128, 128), 0)
    col128 = lax.broadcasted_iota(jnp.int32, (128, 128), 1)
    apart128 = (
        col128 == (row128 & 31) * 4 + (row128 >> 6) * 2 + ((row128 >> 5) & 1)
    ).astype(BF)
    for source, own in ((k_ref, key_own), (v_ref, value_own)):
        parted = jnp.dot(apart128, source[...], preferred_element_type=F32).astype(BF)
        for head in range(2):
            for s in range(2):
                first = head * 64 + s * 32
                own[head, s] = parted[first:first + 32]
    own_head = lax.div(z, 2)
    keys[:, 0, 0, 0, 0] = key_own[own_head]
    values[:, 0, 0, 0, 0] = value_own[own_head]

    def remote(source, target, step, kind, n, device):
        return pltpu.make_async_remote_copy(
            src_ref=source, dst_ref=target, send_sem=kv_send.at[step, kind, n],
            recv_sem=kv_recv.at[step, kind, n], device_id=device, device_id_type=MESH,
        )

    def kv_first():
        for k in (1, 2, 3):
            head = lax.div(lax.rem(z + k, 4), 2)
            remote(key_own.at[head], keys.at[:, 0, k, 0, 0], 0, 0, 0, at(dz=k)).start()
            remote(value_own.at[head], values.at[:, 0, k, 0, 0], 0, 1, 0, at(dz=k)).start()

    def kv_second():
        for k in (2, 1, 3):
            @pl.when(y + k < 4)
            def _():
                remote(keys.at[:, 0, :, 0, 0], keys.at[:, k, :, 0, 0], 1, 0, k, at(dy=k)).start()

            remote(values.at[:, 0, :, 0, 0], values.at[:, 0, :, k, 0], 1, 1, 0, at(dx=k)).start()

    def kv_third():
        for k in (2, 1, 3):
            @pl.when(y + k < 4)
            def _():
                remote(values.at[:, 0, :, :, 0], values.at[:, k, :, :, 0], 2, 1, k, at(dy=k)).start()

        for n in range(4):
            @pl.when(n <= y)
            def _():
                for k in (2, 1, 3):
                    remote(keys.at[:, n, :, 0, 0], keys.at[:, n, :, k, 0], 2, 0, n, at(dx=k)).start()

    def kv_fourth():
        for n in range(4):
            @pl.when(n <= y)
            def _():
                remote(keys.at[:, n, :, :, 0], keys.at[:, n, :, :, 1], 3, 0, n, at(dc=1)).start()
                remote(values.at[:, n, :, :, 0], values.at[:, n, :, :, 1], 3, 1, n, at(dc=1)).start()

    def kv_wait(step, sent):
        def wait(region, kind, n):
            copy = remote(region, region, step, kind, n, at(dc=1))
            if sent:
                copy.wait_send()
            else:
                copy.wait_recv()

        if step == 0:
            wait(keys.at[:, 0, pl.ds(1, 3), 0, 0], 0, 0)
            wait(values.at[:, 0, pl.ds(1, 3), 0, 0], 1, 0)
        if step == 1:
            wait(values.at[:, 0, :, pl.ds(1, 3), 0], 1, 0)
        for n in range(4):
            if step in (1, 2) and n > 0:
                @pl.when(y + n < 4 if sent else n <= y)
                def _():
                    if step == 1:
                        wait(keys.at[:, n, :, 0, 0], 0, n)
                    else:
                        wait(values.at[:, n, :, :, 0], 1, n)

            if step in (2, 3):
                @pl.when(n <= y)
                def _():
                    if step == 2:
                        wait(keys.at[:, n, :, pl.ds(1, 3), 0], 0, n)
                    else:
                        wait(keys.at[:, n, :, :, 1], 0, n)
                        wait(values.at[:, n, :, :, 1], 1, n)

    def sources(stage, j):
        if stage == 0:
            return None, recv_first.at[j]
        if stage == 5:
            return send.at[0, j], recv_last.at[j]
        return send.at[(stage + 1) % 2, j], recv.at[stage - 1, j]

    group_rows = (64, 96, 48, 48, 96, 64)

    def piece(stage, j, group, groups, device):
        source, target = sources(stage, j)
        span = pl.ds(group * group_rows[stage], groups * group_rows[stage])
        if stage == 0:
            source = normed.at[j] if groups == 1 else target.at[span]
        else:
            source = source.at[span]
        return pltpu.make_async_remote_copy(
            src_ref=source, dst_ref=target.at[span],
            send_sem=send_sem.at[stage, j], recv_sem=recv_sem.at[stage, j],
            device_id=device, device_id_type=MESH,
        )

    def along(o, hop, act):
        for n, axes in enumerate(ORDERS):
            pl.when(o == n)(lambda axis="d" + axes[hop]: act(axis))

    def start_hop(stage, j, o):
        hop = stage if stage < 3 else 5 - stage
        sign = 1 if stage < 3 else -1

        def start(axis):
            if hop == 2:
                for k in (4, 5, 2, 6, 3, 7, 1):
                    device = at(**{axis: sign * (k // 2), "dc": k % 2})
                    piece(stage, j, k, 1, device).start()
            else:
                for k in (2, 1, 3):
                    piece(stage, j, k, 1, at(**{axis: sign * k})).start()

        along(o, hop, start)
        rows = group_rows[stage]
        source, target = sources(stage, j)
        if stage == 0:
            target[0:rows] = normed[j]
        else:
            target[0:rows] = source[0:rows]

    def wait_hop(stage, j):
        piece(stage, j, 1, 7 if stage in (2, 3) else 3, at(dc=1)).wait_recv()

    def wait_sent(stage, j):
        piece(stage, j, 1, 7 if stage in (2, 3) else 3, at(dc=1)).wait_send()

    def loop(step, first=0, last=CHUNKS):
        def one(j, carry):
            step(j)
            return carry

        lax.fori_loop(first, last, one, 0)

    def order(j):
        return lax.rem(j, 3)

    pl.semaphore_wait(barrier, len(partners))


    kv_first()
    loop(lambda j: start_hop(0, j, order(j)), 0, 8)

    expert_row = lax.broadcasted_iota(jnp.int32, (128, 32), 0)
    picked_parts, gate_parts = [], []
    for s in range(2):
        picked = jnp.zeros((128, 32), F32)
        gate_of = jnp.zeros((128, 32), F32)
        for k in range(TOPK):
            n = s * TOPK + k
            hit = routes_ref[n:n + 1, :] == expert_row
            picked = picked + jnp.where(hit, 1.0, 0.0)
            gate_of = gate_of + jnp.where(hit, gates_ref[n:n + 1, :], 0.0)
        picked_parts.append(picked)
        gate_parts.append(gate_of)
    picked = jnp.concatenate(picked_parts, axis=1)
    gate_of = jnp.concatenate(gate_parts, axis=1)
    row64 = lax.broadcasted_iota(jnp.int32, (64, 64), 0)
    col64 = lax.broadcasted_iota(jnp.int32, (64, 64), 1)
    position = (col64 >> 3) * 4 + (col64 & 3)
    sequence = (col64 >> 2) & 1
    in_order = (row64 == sequence * 32 + position).astype(BF)
    earlier = ((row64 & 31) * 2 + (row64 >> 5) < position * 2 + sequence).astype(BF)
    gate_high = gate_of.astype(BF)
    gate_low = (gate_of - gate_high.astype(F32)).astype(BF)
    facts = [
        jnp.dot(part, matrix, preferred_element_type=F32).astype(BF)
        for part, matrix in (
            (picked.astype(BF), in_order), (picked.astype(BF), earlier),
            (gate_high, in_order), (gate_low, in_order),
        )
    ]
    def gate_copy(o, group, groups, device):
        span = pl.ds(96 * group, 96 * groups)
        return pltpu.make_async_remote_copy(
            src_ref=gates_own.at[o, span], dst_ref=gates_all.at[o, span],
            send_sem=gate_send.at[o], recv_sem=gate_recv.at[o],
            device_id=device, device_id_type=MESH,
        )

    for o in range(3):
        def target(field):
            return (
                ((y + field(0)) & 3) * 32 + ((z + field(1)) & 3) * 8
                + ((x + field(2)) & 3) * 2 + ((c + field(3)) & 1)
            )

        dest = target(lambda i: cols_ref[:, 8 + o * 8 + i:9 + o * 8 + i])
        hosts = (dest == home_ref[...]).astype(BF)
        named, rank, high, low = [
            jnp.dot(hosts, fact, preferred_element_type=F32) for fact in facts
        ]
        kept = named * jnp.where(
            rank == cols_ref[:, 12 + o * 8:13 + o * 8].astype(F32), 1.0, 0.0
        )
        gates_own[o] = jnp.concatenate([high * kept, low * kept], axis=1).astype(BF)
        gates_all[o, 0:96] = gates_own[o, 0:96]
        for k in (1, 2, 3):
            gate_copy(o, k, 1, at(**{"d" + ORDERS[o][0]: k})).start()

    loop(lambda j: start_hop(0, j, order(j)), 8, 16)
    kv_wait(0, False)
    kv_second()

    lane = lax.broadcasted_iota(jnp.int32, (SLOTS, SLOTS), 1)
    sublane = lax.broadcasted_iota(jnp.int32, (SLOTS, SLOTS), 0)
    for i in (0, 1, 3, 4):
        perm[i] = jnp.where(cols_ref[:, i:i + 1] == lane, 1.0, 0.0).astype(BF)
    perm[2] = jnp.where(rows_ref[0:1, :] == sublane, 1.0, 0.0).astype(BF)

    def reorder(stage, j, matrix):
        for half in range(1):
            span = pl.ds(0, CHUNK)
            send[stage % 2, j, :, span] = jnp.dot(
                perm[matrix], recv[stage - 1, j, :, span], preferred_element_type=F32
            ).astype(BF)

    own_group = (
        lax.broadcasted_iota(jnp.int32, (SLOTS, 256), 1) >> 6
        == lax.div(lax.broadcasted_iota(jnp.int32, (SLOTS, 256), 0), 96)
    )
    for o in range(3):
        gate_copy(o, 1, 3, at(dc=1)).wait_recv()
        high = gates_all[o, :, 0:64].astype(F32)
        filled = jnp.where(
            jnp.logical_and(own_group, jnp.concatenate([high] * 4, axis=1) != 0.0), 1.0, 0.0
        ).astype(BF)
        placing[o] = jnp.dot(perm[0], filled, preferred_element_type=F32).astype(BF)

    def build_gating():
        for o in range(3):
            for n in range(2):
                part = gates_all[o, :, n * 64:(n + 1) * 64].astype(F32)
                spread = jnp.where(own_group, jnp.concatenate([part] * 4, axis=1), 0.0)
                gating[o, n * 256:(n + 1) * 256] = jnp.transpose(
                    jnp.dot(perm[0], spread.astype(BF), preferred_element_type=F32)
                ).astype(BF)

    def second_step(j):
        o = order(j)
        wait_hop(0, j)
        for half in range(1):
            span = pl.ds(0, CHUNK)
            send[0, j, :, span] = jnp.dot(
                placing[o], recv_first[j, :, span], preferred_element_type=F32
            ).astype(BF)
        start_hop(1, j, o)

    def third_step(j):
        o = order(j)
        wait_hop(1, j)
        reorder(1, j, 1)
        start_hop(2, j, o)

    def project_step(j):
        o = order(j)
        wait_hop(2, j)
        slot = lax.rem(j, 2)
        for copy in gate_up_copies(j, slot):
            copy.wait()

        @pl.when(o == 0)
        def _():
            rows_in[...] = recv[1, j]

        @pl.when(o > 0)
        def _():
            rows_in[...] = jnp.dot(
                perm[o + 2], recv[1, j], preferred_element_type=F32
            ).astype(BF)

        for which in range(2):
            for part in range(2):
                span = pl.ds(part * 384, 384)
                hidden_acc[which, :, span] += jnp.dot(
                    rows_in[...], wgu[slot, which, :, span], preferred_element_type=F32
                )

        @pl.when(j + 2 < CHUNKS)
        def _():
            for copy in gate_up_copies(j + 2, slot):
                copy.start()

    loop(second_step, 0, 8)

    apart256 = (col256 == ((row256 & 127) * 2 + (row256 >> 7))).astype(BF)
    for b in range(8):
        parted = jnp.dot(
            apart256, q_ref[b * 256:(b + 1) * 256], preferred_element_type=F32
        ).astype(BF)
        for s in range(2):
            qd[s, b * 128:(b + 1) * 128] = parted[s * 128:(s + 1) * 128]

    hidden_acc[...] = jnp.zeros_like(hidden_acc)
    build_gating()

    def second_third(j):
        second_step(j)
        third_step(j - 8)

    def third_project(j):
        third_step(j)
        project_step(j - 8)

    loop(second_third, 8, 16)
    loop(third_project, 8, 16)
    kv_wait(1, False)
    kv_third()
    loop(project_step, 8, 16)

    gate_proj = hidden_acc[0]
    active[0] = (gate_proj / (1.0 + jnp.exp(-gate_proj)) * hidden_acc[1]).astype(BF)
    down_copy.wait()

    def produce_step(j):
        o = order(j)
        @pl.when(jnp.logical_and(j > 0, j < 3))
        def _():
            back = jnp.where(rows_ref[pl.ds(o + 1, 1), :] == sublane, 1.0, 0.0).astype(BF)
            active[o] = jnp.dot(back, active[0], preferred_element_type=F32).astype(BF)

        wait_sent(1, j)
        span = pl.ds(pl.multiple_of(j * CHUNK, CHUNK), CHUNK)
        send[0, j] = jnp.dot(active[o], wd[:, span], preferred_element_type=F32).astype(BF)
        start_hop(3, j, o)

    loop(produce_step)

    lane_key = lax.broadcasted_iota(jnp.int32, (1, BLOCK), 1)
    key_pos = (
        ((z + 4 - (lane_key >> 8)) & 3) * 256
        + ((x + 4 - ((lane_key >> 6) & 3)) & 3) * 64
        + ((c + (lane_key >> 5)) & 1) * 32
        + (lane_key & 31)
    )
    factor = HEAD_WIDTH ** (-0.5) * 1.4426950408889634

    def attend(t):
        s = lax.div(t, 4)
        first = pl.multiple_of(lax.rem(t, 4) * 256, 256)
        span = pl.ds(first, 256)

        def rows(blocks):
            seen_keys = keys[s, 0:blocks].reshape(blocks * BLOCK, HEAD_WIDTH)
            seen_values = values[s, 0:blocks].reshape(blocks * BLOCK, HEAD_WIDTH)
            scores = lax.dot_general(
                qd[s, span], seen_keys, (((1,), (1,)), ((), ())), preferred_element_type=F32
            )
            query_pos = lax.broadcasted_iota(jnp.int32, (256, 1), 0) + first
            own = jnp.where(key_pos <= query_pos, scores[:, :BLOCK], NEG)
            scores = own if blocks == 1 else jnp.concatenate([own, scores[:, BLOCK:]], axis=1)
            best = jnp.max(scores, axis=-1, keepdims=True) * factor
            weights = jnp.exp2(scores * factor - best)
            total = jnp.sum(weights, axis=-1, keepdims=True)
            ctx_ref[s, span] = (
                jnp.dot(weights.astype(BF), seen_values, preferred_element_type=F32) / total
            ).astype(BF)

        for n in range(4):
            pl.when(y == n)(lambda: rows(n + 1))

    def return_second_step(j):
        wait_hop(3, j)
        wait_sent(2, j)
        reorder(3, j, 2)
        start_hop(4, j, order(j))

    def return_third_step(j):
        wait_hop(4, j)
        wait_sent(3, j)
        o = order(j)
        for half in range(1):
            span = pl.ds(0, CHUNK)
            mixed = jnp.dot(gating[o], recv[3, j, :, span], preferred_element_type=F32)
            send[0, j, 0:256, span] = (mixed[:256] + mixed[256:]).astype(BF)
        start_hop(5, j, o)

    def combine_step(j):
        wait_hop(5, j)
        span = pl.ds(pl.multiple_of(j * CHUNK, CHUNK), CHUNK)
        parts = [recv_last[j, k * 64:(k + 1) * 64].astype(F32) for k in range(4)]
        out_ref[:, span] += (parts[0] + parts[1]) + (parts[2] + parts[3])

    def first_back(j):
        return_second_step(j)

        @pl.when(j == 4)
        def _():
            kv_wait(2, False)
            kv_fourth()

        pl.when(j == 8)(lambda: kv_wait(3, False))
        pl.when(jnp.logical_and(j >= 12, j < 13))(lambda: attend(j - 12))

    loop(first_back)

    def second_back(j):
        return_third_step(j)
        due = lax.rem(j, 4) == 0
        pl.when(due)(lambda: attend(lax.div(j, 4) + 1))

    loop(second_back)

    loop(attend, 5, 7)

    def third_back(j):
        combine_step(j)
        pl.when(jnp.logical_and(j >= 6, j < 7))(lambda: attend(j + 1))

    loop(third_back)

    def drain_step(j):
        wait_sent(0, j)
        wait_sent(4, j)
        wait_sent(5, j)

    loop(drain_step)
    for o in range(3):
        gate_copy(o, 1, 3, at(dc=1)).wait_send()
    for step in range(4):
        kv_wait(step, True)


def tile_rows(array):
    parts = array.reshape(array.shape[0], 2, -1, 128).transpose(0, 2, 1, 3)
    return parts.reshape(-1, 128)


def finish_kernel(parted_ref, tokens_ref, ctx_ref, out_ref):
    row = lax.broadcasted_iota(jnp.int32, (256, 256), 0)
    col = lax.broadcasted_iota(jnp.int32, (256, 256), 1)
    together = (col == ((row & 1) * 128 + (row >> 1))).astype(BF)
    for b in range(8):
        span = slice(b * 128, (b + 1) * 128)
        both = jnp.concatenate([parted_ref[s, span] for s in range(2)], axis=0)
        ctx_ref[b * 256:(b + 1) * 256] = jnp.dot(
            together, both, preferred_element_type=F32
        ).astype(BF)
    tiles = (col == ((row & 63) >> 1) * 8 + (row & 1) * 4 + (row >> 6)).astype(BF)
    for b in range(8):
        block = jnp.concatenate(
            [tokens_ref[b * 8:(b + 1) * 8, n * 128:(n + 1) * 128] for n in range(32)], axis=0
        ).astype(BF)
        out_ref[b * 256:(b + 1) * 256] = jnp.dot(
            tiles, block, preferred_element_type=F32
        ).astype(BF)


def body(
    queries, key_rows, values, hidden, norm_gain, routes, route_gates, expert_home,
    w_gate, w_up, w_down,
):
    columns, rows = slot_tables()
    vmem = pl.BlockSpec(memory_space=pltpu.VMEM)
    hbm = pl.BlockSpec(memory_space=pl.ANY)
    block = (CHUNKS, SLOTS, CHUNK)
    parted, tokens = pl.pallas_call(
        kernel,
        out_shape=(
            jax.ShapeDtypeStruct((2, BLOCK, HEAD_WIDTH), BF),
            jax.ShapeDtypeStruct((TOKENS, WIDTH), F32),
        ),
        in_specs=[vmem] * 10 + [hbm] * 3,
        out_specs=(vmem, vmem),
        scratch_shapes=[
            pltpu.VMEM((2,) + block, BF),
            pltpu.VMEM((4,) + block, BF),
            pltpu.VMEM((CHUNKS, 4 * TOKENS, CHUNK), BF),
            pltpu.VMEM((CHUNKS, 4 * TOKENS, CHUNK), BF),
            pltpu.VMEM((2, 2, CHUNK, FF), BF),
            pltpu.VMEM((FF, WIDTH), BF),
            pltpu.VMEM((5, SLOTS, SLOTS), BF),
            pltpu.VMEM((CHUNKS, TOKENS, CHUNK), BF),
            pltpu.VMEM((3, SLOTS, 2 * TOKENS), BF),
            pltpu.VMEM((3, SLOTS, 2 * TOKENS), BF),
            pltpu.VMEM((3, SLOTS, 4 * TOKENS), BF),
            pltpu.VMEM((3, 8 * TOKENS, SLOTS), BF),
            pltpu.VMEM((2, SLOTS, FF), F32),
            pltpu.VMEM((SLOTS, CHUNK), BF),
            pltpu.VMEM((3, SLOTS, FF), BF),
            pltpu.VMEM((2, 2, 32, HEAD_WIDTH), BF),
            pltpu.VMEM((2, 2, 32, HEAD_WIDTH), BF),
            pltpu.VMEM((2, 4, 4, 4, 2, 32, HEAD_WIDTH), BF),
            pltpu.VMEM((2, 4, 4, 4, 2, 32, HEAD_WIDTH), BF),
            pltpu.VMEM((2, BLOCK, HEAD_WIDTH), BF),
            pltpu.SemaphoreType.DMA((6, CHUNKS)),
            pltpu.SemaphoreType.DMA((6, CHUNKS)),
            pltpu.SemaphoreType.DMA((3,)),
            pltpu.SemaphoreType.DMA((3,)),
            pltpu.SemaphoreType.DMA((3, 2)),
            pltpu.SemaphoreType.DMA((4, 2, 4)),
            pltpu.SemaphoreType.DMA((4, 2, 4)),
        ],
        compiler_params=pltpu.CompilerParams(
            collective_id=0, has_side_effects=True, vmem_limit_bytes=62 * 2**20
        ),
    )(
        queries.reshape(2 * BLOCK, HEAD_WIDTH),
        tile_rows(key_rows),
        tile_rows(values),
        tile_rows(hidden),
        norm_gain.reshape(1, WIDTH),
        routes.transpose(1, 2, 0).reshape(2 * TOPK, -1),
        route_gates.transpose(1, 2, 0).reshape(2 * TOPK, -1),
        expert_home.reshape(1, 128),
        jnp.asarray(columns),
        jnp.asarray(rows),
        w_gate[0],
        w_up[0],
        w_down[0],
    )
    context, layer_out = pl.pallas_call(
        finish_kernel,
        out_shape=(
            jax.ShapeDtypeStruct((2 * BLOCK, HEAD_WIDTH), BF),
            jax.ShapeDtypeStruct((TOKENS * WIDTH // 128, 128), BF),
        ),
        in_specs=[vmem, vmem],
        out_specs=(vmem, vmem),
    )(parted, tokens)
    layer_out = layer_out.reshape(-1, WIDTH // 128, 2, 128).transpose(0, 2, 1, 3)
    return context.reshape(queries.shape), layer_out.reshape(hidden.shape)


def solution(mesh):
    both = P(("ctx", "exp"), None, None)
    in_specs = (P("ctx", None, "exp"), both, both, both, P(), both, both, P(), both, both, both)
    out_specs = (P("ctx", None, "exp"), both)
    return jax.shard_map(body, mesh=mesh, in_specs=in_specs, out_specs=out_specs, check_vma=False)
```

```python
import jax
import jax.numpy as jnp
import numpy as np
from jax import lax
from jax.experimental import pallas as pl
from jax.experimental.pallas import tpu as pltpu
from jax.sharding import PartitionSpec as P

MESH = pl.DeviceIdType.MESH
HEAD_WIDTH = 128
TOPK = 8
WIDTH = 4096
FF = 768
CAP = 3
TOKENS = 64
SLOTS = 384
CHUNKS = 16
CHUNK = WIDTH // CHUNKS
BLOCK = 1024
ORDERS = (("y", "z", "x"), ("z", "x", "y"), ("x", "y", "z"))
NEG = -1e30
BF = jnp.bfloat16
F32 = jnp.float32


def slot_tables():
    grids = np.indices((4, 4, 8, CAP)).reshape(4, SLOTS)

    def index(new, old, sizes):
        where = np.zeros(SLOTS, np.int32)
        where[np.ravel_multi_index(old, sizes)] = np.arange(SLOTS)
        return where[np.ravel_multi_index(new, sizes)]

    by_start = list(grids)
    by_middle = np.indices((4, 4, 8, CAP)).reshape(4, SLOTS)[[1, 0, 2, 3]]
    by_end = np.indices((8, 4, 4, CAP)).reshape(4, SLOTS)[[2, 1, 0, 3]]
    sizes = (4, 4, 8, CAP)
    columns = np.zeros((SLOTS, 128), np.int32)
    rows = np.zeros((8, SLOTS), np.int32)
    columns[:, 0] = index(by_middle, by_start, sizes)
    columns[:, 1] = index(by_end, by_middle, sizes)
    rows[0] = columns[:, 1]

    def offsets(keys, axes):
        found = dict(zip(axes, (keys[0], keys[1], keys[2] // 2)))
        return [found["y"], found["z"], found["x"], keys[2] % 2, keys[3]]

    common = offsets(by_end, ORDERS[0])
    for o, axes in enumerate(ORDERS):
        for i, entry in enumerate(offsets(by_start, axes)):
            columns[:, 8 + o * 8 + i] = entry
        rows[1 + o] = index(common, offsets(by_end, axes), (4, 4, 4, 2, CAP))
        columns[:, 2 + o] = rows[1 + o]
    return columns, rows


def kernel(
    q_ref, k_ref, v_ref, hid_ref, gain_ref, routes_ref, gates_ref, home_ref,
    cols_ref, rows_ref, wg_hbm, wu_hbm, wd_hbm,
    ctx_ref, out_ref,
    send, recv, recv_first, recv_last, wgu, wd, perm, normed, gates_own, gates_all, placing,
    gating, hidden_acc, rows_in, active,
    key_own, value_own, keys, values, qd,
    send_sem, recv_sem, gate_send, gate_recv, weight_sem, kv_send, kv_recv,
):
    y = lax.axis_index("ctx")
    flat = lax.axis_index("exp")
    z = lax.div(flat, 8)
    w = lax.rem(flat, 8)
    x = lax.div(w, 2)
    c = lax.rem(w, 2)

    def at(dy=0, dz=0, dx=0, dc=0):
        return (
            lax.rem(y + (dy + 4), 4),
            lax.rem(z + (dz + 4), 4) * 8 + lax.rem(x + (dx + 4), 4) * 2 + lax.rem(c + dc, 2),
        )

    barrier = pltpu.get_barrier_semaphore()
    partners = [at(dc=1)]
    for axis in ("dy", "dz", "dx"):
        partners += [at(**{axis: k, "dc": n}) for k in (1, 2, 3) for n in (0, 1)]
    for partner in partners:
        pl.semaphore_signal(barrier, inc=1, device_id=partner, device_id_type=MESH)

    def gate_up_copies(j, slot):
        span = pl.ds(pl.multiple_of(j * CHUNK, CHUNK), CHUNK)
        return (
            pltpu.make_async_copy(wg_hbm.at[span], wgu.at[slot, 0], weight_sem.at[slot, 0]),
            pltpu.make_async_copy(wu_hbm.at[span], wgu.at[slot, 1], weight_sem.at[slot, 1]),
        )

    for slot in range(2):
        for copy in gate_up_copies(slot, slot):
            copy.start()
    down_copy = pltpu.make_async_copy(wd_hbm, wd, weight_sem.at[2, 0])
    down_copy.start()

    row256 = lax.broadcasted_iota(jnp.int32, (256, 256), 0)
    col256 = lax.broadcasted_iota(jnp.int32, (256, 256), 1)
    apart_tiles = (
        col256 == (row256 & 3) * 64 + (row256 >> 3) * 2 + ((row256 >> 2) & 1)
    ).astype(BF)
    for b in range(8):
        parted = jnp.dot(
            apart_tiles, hid_ref[b * 256:(b + 1) * 256], preferred_element_type=F32
        )
        for tile in range(32):
            out_ref[b * 8:(b + 1) * 8, tile * 128:(tile + 1) * 128] = (
                parted[tile * 8:(tile + 1) * 8]
            )

    tokens = out_ref[...]
    scale = lax.rsqrt(jnp.mean(tokens * tokens, axis=-1, keepdims=True) + 1e-06)
    for j in range(CHUNKS):
        span = slice(j * CHUNK, (j + 1) * CHUNK)
        normed[j] = (out_ref[:, span] * scale * gain_ref[:, span]).astype(BF)

    row128 = lax.broadcasted_iota(jnp.int32, (128, 128), 0)
    col128 = lax.broadcasted_iota(jnp.int32, (128, 128), 1)
    apart128 = (
        col128 == (row128 & 31) * 4 + (row128 >> 6) * 2 + ((row128 >> 5) & 1)
    ).astype(BF)
    for source, own in ((k_ref, key_own), (v_ref, value_own)):
        parted = jnp.dot(apart128, source[...], preferred_element_type=F32).astype(BF)
        for head in range(2):
            for s in range(2):
                first = head * 64 + s * 32
                own[head, s] = parted[first:first + 32]
    own_head = lax.div(z, 2)
    keys[:, 0, 0, 0, 0] = key_own[own_head]
    values[:, 0, 0, 0, 0] = value_own[own_head]

    def remote(source, target, step, kind, n, device):
        return pltpu.make_async_remote_copy(
            src_ref=source, dst_ref=target, send_sem=kv_send.at[step, kind, n],
            recv_sem=kv_recv.at[step, kind, n], device_id=device, device_id_type=MESH,
        )

    def kv_first():
        for k in (1, 2, 3):
            head = lax.div(lax.rem(z + k, 4), 2)
            remote(key_own.at[head], keys.at[:, 0, k, 0, 0], 0, 0, 0, at(dz=k)).start()
            remote(value_own.at[head], values.at[:, 0, k, 0, 0], 0, 1, 0, at(dz=k)).start()

    def kv_second():
        for k in (2, 1, 3):
            @pl.when(y + k < 4)
            def _():
                remote(keys.at[:, 0, :, 0, 0], keys.at[:, k, :, 0, 0], 1, 0, k, at(dy=k)).start()

            remote(values.at[:, 0, :, 0, 0], values.at[:, 0, :, k, 0], 1, 1, 0, at(dx=k)).start()

    def kv_third():
        for k in (2, 1, 3):
            @pl.when(y + k < 4)
            def _():
                remote(values.at[:, 0, :, :, 0], values.at[:, k, :, :, 0], 2, 1, k, at(dy=k)).start()

        for n in range(4):
            @pl.when(n <= y)
            def _():
                for k in (2, 1, 3):
                    remote(keys.at[:, n, :, 0, 0], keys.at[:, n, :, k, 0], 2, 0, n, at(dx=k)).start()

    def kv_fourth():
        for n in range(4):
            @pl.when(n <= y)
            def _():
                remote(keys.at[:, n, :, :, 0], keys.at[:, n, :, :, 1], 3, 0, n, at(dc=1)).start()
                remote(values.at[:, n, :, :, 0], values.at[:, n, :, :, 1], 3, 1, n, at(dc=1)).start()

    def kv_wait(step, sent):
        def wait(region, kind, n):
            copy = remote(region, region, step, kind, n, at(dc=1))
            if sent:
                copy.wait_send()
            else:
                copy.wait_recv()

        if step == 0:
            wait(keys.at[:, 0, pl.ds(1, 3), 0, 0], 0, 0)
            wait(values.at[:, 0, pl.ds(1, 3), 0, 0], 1, 0)
        if step == 1:
            wait(values.at[:, 0, :, pl.ds(1, 3), 0], 1, 0)
        for n in range(4):
            if step in (1, 2) and n > 0:
                @pl.when(y + n < 4 if sent else n <= y)
                def _():
                    if step == 1:
                        wait(keys.at[:, n, :, 0, 0], 0, n)
                    else:
                        wait(values.at[:, n, :, :, 0], 1, n)

            if step in (2, 3):
                @pl.when(n <= y)
                def _():
                    if step == 2:
                        wait(keys.at[:, n, :, pl.ds(1, 3), 0], 0, n)
                    else:
                        wait(keys.at[:, n, :, :, 1], 0, n)
                        wait(values.at[:, n, :, :, 1], 1, n)

    def sources(stage, j):
        if stage == 0:
            return None, recv_first.at[j]
        if stage == 5:
            return send.at[0, j], recv_last.at[j]
        return send.at[(stage + 1) % 2, j], recv.at[stage - 1, j]

    group_rows = (64, 96, 48, 48, 96, 64)

    def piece(stage, j, group, groups, device):
        source, target = sources(stage, j)
        span = pl.ds(group * group_rows[stage], groups * group_rows[stage])
        if stage == 0:
            source = normed.at[j] if groups == 1 else target.at[span]
        else:
            source = source.at[span]
        return pltpu.make_async_remote_copy(
            src_ref=source, dst_ref=target.at[span],
            send_sem=send_sem.at[stage, j], recv_sem=recv_sem.at[stage, j],
            device_id=device, device_id_type=MESH,
        )

    def along(o, hop, act):
        for n, axes in enumerate(ORDERS):
            pl.when(o == n)(lambda axis="d" + axes[hop]: act(axis))

    def start_hop(stage, j, o):
        hop = stage if stage < 3 else 5 - stage
        sign = 1 if stage < 3 else -1

        def start(axis):
            if hop == 2:
                for k in (2, 6, 3, 7, 4, 5, 1):
                    device = at(**{axis: sign * (k // 2), "dc": k % 2})
                    piece(stage, j, k, 1, device).start()
            else:
                for k in (1, 3, 2):
                    piece(stage, j, k, 1, at(**{axis: sign * k})).start()

        along(o, hop, start)
        rows = group_rows[stage]
        source, target = sources(stage, j)
        if stage == 0:
            target[0:rows] = normed[j]
        else:
            target[0:rows] = source[0:rows]

    def wait_hop(stage, j):
        piece(stage, j, 1, 7 if stage in (2, 3) else 3, at(dc=1)).wait_recv()

    def wait_sent(stage, j):
        piece(stage, j, 1, 7 if stage in (2, 3) else 3, at(dc=1)).wait_send()

    def loop(step, first=0, last=CHUNKS):
        def one(j, carry):
            step(j)
            return carry

        lax.fori_loop(first, last, one, 0)

    def order(j):
        return lax.rem(j, 3)

    pl.semaphore_wait(barrier, len(partners))


    kv_first()
    loop(lambda j: start_hop(0, j, order(j)), 0, 8)

    expert_row = lax.broadcasted_iota(jnp.int32, (128, 32), 0)
    picked_parts, gate_parts = [], []
    for s in range(2):
        picked = jnp.zeros((128, 32), F32)
        gate_of = jnp.zeros((128, 32), F32)
        for k in range(TOPK):
            n = s * TOPK + k
            hit = routes_ref[n:n + 1, :] == expert_row
            picked = picked + jnp.where(hit, 1.0, 0.0)
            gate_of = gate_of + jnp.where(hit, gates_ref[n:n + 1, :], 0.0)
        picked_parts.append(picked)
        gate_parts.append(gate_of)
    picked = jnp.concatenate(picked_parts, axis=1)
    gate_of = jnp.concatenate(gate_parts, axis=1)
    row64 = lax.broadcasted_iota(jnp.int32, (64, 64), 0)
    col64 = lax.broadcasted_iota(jnp.int32, (64, 64), 1)
    position = (col64 >> 3) * 4 + (col64 & 3)
    sequence = (col64 >> 2) & 1
    in_order = (row64 == sequence * 32 + position).astype(BF)
    earlier = ((row64 & 31) * 2 + (row64 >> 5) < position * 2 + sequence).astype(BF)
    gate_high = gate_of.astype(BF)
    gate_low = (gate_of - gate_high.astype(F32)).astype(BF)
    facts = [
        jnp.dot(part, matrix, preferred_element_type=F32).astype(BF)
        for part, matrix in (
            (picked.astype(BF), in_order), (picked.astype(BF), earlier),
            (gate_high, in_order), (gate_low, in_order),
        )
    ]
    def gate_copy(o, group, groups, device):
        span = pl.ds(96 * group, 96 * groups)
        return pltpu.make_async_remote_copy(
            src_ref=gates_own.at[o, span], dst_ref=gates_all.at[o, span],
            send_sem=gate_send.at[o], recv_sem=gate_recv.at[o],
            device_id=device, device_id_type=MESH,
        )

    for o in range(3):
        def target(field):
            return (
                ((y + field(0)) & 3) * 32 + ((z + field(1)) & 3) * 8
                + ((x + field(2)) & 3) * 2 + ((c + field(3)) & 1)
            )

        dest = target(lambda i: cols_ref[:, 8 + o * 8 + i:9 + o * 8 + i])
        hosts = (dest == home_ref[...]).astype(BF)
        named, rank, high, low = [
            jnp.dot(hosts, fact, preferred_element_type=F32) for fact in facts
        ]
        kept = named * jnp.where(
            rank == cols_ref[:, 12 + o * 8:13 + o * 8].astype(F32), 1.0, 0.0
        )
        gates_own[o] = jnp.concatenate([high * kept, low * kept], axis=1).astype(BF)
        gates_all[o, 0:96] = gates_own[o, 0:96]
        for k in (1, 2, 3):
            gate_copy(o, k, 1, at(**{"d" + ORDERS[o][0]: k})).start()

    loop(lambda j: start_hop(0, j, order(j)), 8, 16)
    kv_wait(0, False)
    kv_second()

    lane = lax.broadcasted_iota(jnp.int32, (SLOTS, SLOTS), 1)
    sublane = lax.broadcasted_iota(jnp.int32, (SLOTS, SLOTS), 0)
    for i in (0, 1, 3, 4):
        perm[i] = jnp.where(cols_ref[:, i:i + 1] == lane, 1.0, 0.0).astype(BF)
    perm[2] = jnp.where(rows_ref[0:1, :] == sublane, 1.0, 0.0).astype(BF)

    def reorder(stage, j, matrix):
        for half in range(1):
            span = pl.ds(0, CHUNK)
            send[stage % 2, j, :, span] = jnp.dot(
                perm[matrix], recv[stage - 1, j, :, span], preferred_element_type=F32
            ).astype(BF)

    own_group = (
        lax.broadcasted_iota(jnp.int32, (SLOTS, 256), 1) >> 6
        == lax.div(lax.broadcasted_iota(jnp.int32, (SLOTS, 256), 0), 96)
    )
    for o in range(3):
        gate_copy(o, 1, 3, at(dc=1)).wait_recv()
        high = gates_all[o, :, 0:64].astype(F32)
        filled = jnp.where(
            jnp.logical_and(own_group, jnp.concatenate([high] * 4, axis=1) != 0.0), 1.0, 0.0
        ).astype(BF)
        placing[o] = jnp.dot(perm[0], filled, preferred_element_type=F32).astype(BF)

    def build_gating():
        for o in range(3):
            for n in range(2):
                part = gates_all[o, :, n * 64:(n + 1) * 64].astype(F32)
                spread = jnp.where(own_group, jnp.concatenate([part] * 4, axis=1), 0.0)
                gating[o, n * 256:(n + 1) * 256] = jnp.transpose(
                    jnp.dot(perm[0], spread.astype(BF), preferred_element_type=F32)
                ).astype(BF)

    def second_step(j):
        o = order(j)
        wait_hop(0, j)
        for half in range(1):
            span = pl.ds(0, CHUNK)
            send[0, j, :, span] = jnp.dot(
                placing[o], recv_first[j, :, span], preferred_element_type=F32
            ).astype(BF)
        start_hop(1, j, o)

    def third_step(j):
        o = order(j)
        wait_hop(1, j)
        reorder(1, j, 1)
        start_hop(2, j, o)

    def project_step(j):
        o = order(j)
        wait_hop(2, j)
        slot = lax.rem(j, 2)
        for copy in gate_up_copies(j, slot):
            copy.wait()

        @pl.when(o == 0)
        def _():
            rows_in[...] = recv[1, j]

        @pl.when(o > 0)
        def _():
            rows_in[...] = jnp.dot(
                perm[o + 2], recv[1, j], preferred_element_type=F32
            ).astype(BF)

        for which in range(2):
            for part in range(2):
                span = pl.ds(part * 384, 384)
                hidden_acc[which, :, span] += jnp.dot(
                    rows_in[...], wgu[slot, which, :, span], preferred_element_type=F32
                )

        @pl.when(j + 2 < CHUNKS)
        def _():
            for copy in gate_up_copies(j + 2, slot):
                copy.start()

    loop(second_step, 0, 8)

    apart256 = (col256 == ((row256 & 127) * 2 + (row256 >> 7))).astype(BF)
    for b in range(8):
        parted = jnp.dot(
            apart256, q_ref[b * 256:(b + 1) * 256], preferred_element_type=F32
        ).astype(BF)
        for s in range(2):
            qd[s, b * 128:(b + 1) * 128] = parted[s * 128:(s + 1) * 128]

    hidden_acc[...] = jnp.zeros_like(hidden_acc)
    build_gating()

    def second_third(j):
        second_step(j)
        third_step(j - 8)

    def third_project(j):
        third_step(j)
        project_step(j - 8)

    loop(second_third, 8, 16)
    loop(third_project, 8, 16)
    kv_wait(1, False)
    kv_third()
    loop(project_step, 8, 16)

    gate_proj = hidden_acc[0]
    active[0] = (gate_proj / (1.0 + jnp.exp(-gate_proj)) * hidden_acc[1]).astype(BF)
    down_copy.wait()

    def produce_step(j):
        o = order(j)
        @pl.when(jnp.logical_and(j > 0, j < 3))
        def _():
            back = jnp.where(rows_ref[pl.ds(o + 1, 1), :] == sublane, 1.0, 0.0).astype(BF)
            active[o] = jnp.dot(back, active[0], preferred_element_type=F32).astype(BF)

        wait_sent(1, j)
        span = pl.ds(pl.multiple_of(j * CHUNK, CHUNK), CHUNK)
        send[0, j] = jnp.dot(active[o], wd[:, span], preferred_element_type=F32).astype(BF)
        start_hop(3, j, o)

    loop(produce_step)

    lane_key = lax.broadcasted_iota(jnp.int32, (1, BLOCK), 1)
    key_pos = (
        ((z + 4 - (lane_key >> 8)) & 3) * 256
        + ((x + 4 - ((lane_key >> 6) & 3)) & 3) * 64
        + ((c + (lane_key >> 5)) & 1) * 32
        + (lane_key & 31)
    )
    factor = HEAD_WIDTH ** (-0.5) * 1.4426950408889634

    def attend(t):
        s = lax.div(t, 4)
        first = pl.multiple_of(lax.rem(t, 4) * 256, 256)
        span = pl.ds(first, 256)

        def rows(blocks):
            seen_keys = keys[s, 0:blocks].reshape(blocks * BLOCK, HEAD_WIDTH)
            seen_values = values[s, 0:blocks].reshape(blocks * BLOCK, HEAD_WIDTH)
            scores = lax.dot_general(
                qd[s, span], seen_keys, (((1,), (1,)), ((), ())), preferred_element_type=F32
            )
            query_pos = lax.broadcasted_iota(jnp.int32, (256, 1), 0) + first
            own = jnp.where(key_pos <= query_pos, scores[:, :BLOCK], NEG)
            scores = own if blocks == 1 else jnp.concatenate([own, scores[:, BLOCK:]], axis=1)
            best = jnp.max(scores, axis=-1, keepdims=True) * factor
            weights = jnp.exp2(scores * factor - best)
            total = jnp.sum(weights, axis=-1, keepdims=True)
            ctx_ref[s, span] = (
                jnp.dot(weights.astype(BF), seen_values, preferred_element_type=F32) / total
            ).astype(BF)

        for n in range(4):
            pl.when(y == n)(lambda: rows(n + 1))

    def return_second_step(j):
        wait_hop(3, j)
        wait_sent(2, j)
        reorder(3, j, 2)
        start_hop(4, j, order(j))

    def return_third_step(j):
        wait_hop(4, j)
        wait_sent(3, j)
        o = order(j)
        for half in range(1):
            span = pl.ds(0, CHUNK)
            mixed = jnp.dot(gating[o], recv[3, j, :, span], preferred_element_type=F32)
            send[0, j, 0:256, span] = (mixed[:256] + mixed[256:]).astype(BF)
        start_hop(5, j, o)

    def combine_step(j):
        wait_hop(5, j)
        span = pl.ds(pl.multiple_of(j * CHUNK, CHUNK), CHUNK)
        parts = [recv_last[j, k * 64:(k + 1) * 64].astype(F32) for k in range(4)]
        out_ref[:, span] += (parts[0] + parts[1]) + (parts[2] + parts[3])

    def first_back(j):
        return_second_step(j)

        @pl.when(j == 2)
        def _():
            kv_wait(2, False)
            kv_fourth()

        pl.when(j == 6)(lambda: kv_wait(3, False))
        pl.when(jnp.logical_or(j == 8, j == 12))(lambda: attend(lax.div(j, 4) - 2))

    loop(first_back)

    def second_back(j):
        return_third_step(j)
        due = lax.rem(j, 4) == 0
        pl.when(due)(lambda: attend(lax.div(j, 4) + 2))

    loop(second_back)

    loop(attend, 6, 7)

    def third_back(j):
        combine_step(j)
        pl.when(jnp.logical_and(j >= 6, j < 7))(lambda: attend(j + 1))

    loop(third_back)

    def drain_step(j):
        wait_sent(0, j)
        wait_sent(4, j)
        wait_sent(5, j)

    loop(drain_step)
    for o in range(3):
        gate_copy(o, 1, 3, at(dc=1)).wait_send()
    for step in range(4):
        kv_wait(step, True)


def tile_rows(array):
    parts = array.reshape(array.shape[0], 2, -1, 128).transpose(0, 2, 1, 3)
    return parts.reshape(-1, 128)


def finish_kernel(parted_ref, tokens_ref, ctx_ref, out_ref):
    row = lax.broadcasted_iota(jnp.int32, (256, 256), 0)
    col = lax.broadcasted_iota(jnp.int32, (256, 256), 1)
    together = (col == ((row & 1) * 128 + (row >> 1))).astype(BF)
    for b in range(8):
        span = slice(b * 128, (b + 1) * 128)
        both = jnp.concatenate([parted_ref[s, span] for s in range(2)], axis=0)
        ctx_ref[b * 256:(b + 1) * 256] = jnp.dot(
            together, both, preferred_element_type=F32
        ).astype(BF)
    tiles = (col == ((row & 63) >> 1) * 8 + (row & 1) * 4 + (row >> 6)).astype(BF)
    for b in range(8):
        block = jnp.concatenate(
            [tokens_ref[b * 8:(b + 1) * 8, n * 128:(n + 1) * 128] for n in range(32)], axis=0
        ).astype(BF)
        out_ref[b * 256:(b + 1) * 256] = jnp.dot(
            tiles, block, preferred_element_type=F32
        ).astype(BF)


def body(
    queries, key_rows, values, hidden, norm_gain, routes, route_gates, expert_home,
    w_gate, w_up, w_down,
):
    columns, rows = slot_tables()
    vmem = pl.BlockSpec(memory_space=pltpu.VMEM)
    hbm = pl.BlockSpec(memory_space=pl.ANY)
    block = (CHUNKS, SLOTS, CHUNK)
    parted, tokens = pl.pallas_call(
        kernel,
        out_shape=(
            jax.ShapeDtypeStruct((2, BLOCK, HEAD_WIDTH), BF),
            jax.ShapeDtypeStruct((TOKENS, WIDTH), F32),
        ),
        in_specs=[vmem] * 10 + [hbm] * 3,
        out_specs=(vmem, vmem),
        scratch_shapes=[
            pltpu.VMEM((2,) + block, BF),
            pltpu.VMEM((4,) + block, BF),
            pltpu.VMEM((CHUNKS, 4 * TOKENS, CHUNK), BF),
            pltpu.VMEM((CHUNKS, 4 * TOKENS, CHUNK), BF),
            pltpu.VMEM((2, 2, CHUNK, FF), BF),
            pltpu.VMEM((FF, WIDTH), BF),
            pltpu.VMEM((5, SLOTS, SLOTS), BF),
            pltpu.VMEM((CHUNKS, TOKENS, CHUNK), BF),
            pltpu.VMEM((3, SLOTS, 2 * TOKENS), BF),
            pltpu.VMEM((3, SLOTS, 2 * TOKENS), BF),
            pltpu.VMEM((3, SLOTS, 4 * TOKENS), BF),
            pltpu.VMEM((3, 8 * TOKENS, SLOTS), BF),
            pltpu.VMEM((2, SLOTS, FF), F32),
            pltpu.VMEM((SLOTS, CHUNK), BF),
            pltpu.VMEM((3, SLOTS, FF), BF),
            pltpu.VMEM((2, 2, 32, HEAD_WIDTH), BF),
            pltpu.VMEM((2, 2, 32, HEAD_WIDTH), BF),
            pltpu.VMEM((2, 4, 4, 4, 2, 32, HEAD_WIDTH), BF),
            pltpu.VMEM((2, 4, 4, 4, 2, 32, HEAD_WIDTH), BF),
            pltpu.VMEM((2, BLOCK, HEAD_WIDTH), BF),
            pltpu.SemaphoreType.DMA((6, CHUNKS)),
            pltpu.SemaphoreType.DMA((6, CHUNKS)),
            pltpu.SemaphoreType.DMA((3,)),
            pltpu.SemaphoreType.DMA((3,)),
            pltpu.SemaphoreType.DMA((3, 2)),
            pltpu.SemaphoreType.DMA((4, 2, 4)),
            pltpu.SemaphoreType.DMA((4, 2, 4)),
        ],
        compiler_params=pltpu.CompilerParams(
            collective_id=0, has_side_effects=True, vmem_limit_bytes=62 * 2**20
        ),
    )(
        queries.reshape(2 * BLOCK, HEAD_WIDTH),
        tile_rows(key_rows),
        tile_rows(values),
        tile_rows(hidden),
        norm_gain.reshape(1, WIDTH),
        routes.transpose(1, 2, 0).reshape(2 * TOPK, -1),
        route_gates.transpose(1, 2, 0).reshape(2 * TOPK, -1),
        expert_home.reshape(1, 128),
        jnp.asarray(columns),
        jnp.asarray(rows),
        w_gate[0],
        w_up[0],
        w_down[0],
    )
    context, layer_out = pl.pallas_call(
        finish_kernel,
        out_shape=(
            jax.ShapeDtypeStruct((2 * BLOCK, HEAD_WIDTH), BF),
            jax.ShapeDtypeStruct((TOKENS * WIDTH // 128, 128), BF),
        ),
        in_specs=[vmem, vmem],
        out_specs=(vmem, vmem),
    )(parted, tokens)
    layer_out = layer_out.reshape(-1, WIDTH // 128, 2, 128).transpose(0, 2, 1, 3)
    return context.reshape(queries.shape), layer_out.reshape(hidden.shape)


def solution(mesh):
    both = P(("ctx", "exp"), None, None)
    in_specs = (P("ctx", None, "exp"), both, both, both, P(), both, both, P(), both, both, both)
    out_specs = (P("ctx", None, "exp"), both)
    return jax.shard_map(body, mesh=mesh, in_specs=in_specs, out_specs=out_specs, check_vma=False)
```
